128 devices in a mesh: tm: 4 (over x), space: 32 (over z, y, core).
Axes of the slice: x: 4, y: 4, z: 4, core: 2. Of those that a mesh axis runs over, the one named last changes fastest.
Arguments:
- initial: float32 [3, 1024, 1024], P(None, 'space'), may hold values from -6 to 6
- guess: float32 [8, 3, 1024, 1024], P('tm', None, 'space'), may hold values from -6 to 6
- depth: float32 [1024, 1024], P('space'), may hold values from 0.2 to 1
- friction: float32 [1024, 1024], P('space'), may hold values from 0.005 to 0.1
- mask: int32 [1024, 1024], P('space'), may hold values 0 or 1
- wind: float32 [8, 2, 1024, 1024], P('tm', None, 'space'), may hold values from -6 to 6
Outputs:
- corrected: float32 [8, 3, 1024, 1024], P('tm', None, 'space')
The draws below stay inside these ranges and needn't reach their ends.
Inputs may be any that keep to these rules, and one draw needn't show every extreme that they name: `mask`: 1 marks a sea cell, 0 a land cell.
All inputs are finite; a program needn't handle non-finite values. No bound on the sum of `mask` on one device may be relied on, other than what follows from the above.
Results may differ from the reference program's by a relative error of at most 0.000039.
Values sent between devices are 32-bit elements; how exact they have to be, the bound alone decides.
No kernel may reach another device: no remote copies, remote signals or barrier semaphores. Data moves between devices by JAX's collectives and lax.ppermute only.
A program may use at most 64 MiB of HBM per device.

```python
import math
import jax
import jax.numpy as jnp
from jax import lax

NX = 1024
FACTOR = 16
NY = 1024
INTERVALS = 8


def with_ends(array, key, low, top_value):
    longest = array.shape.index(max(array.shape))
    spots = []
    for shift in (0, 1):
        where = [jax.random.randint(jax.random.fold_in(key, axis), (), 0, length) for axis, length in enumerate(array.shape)]
        where[longest] = (where[longest] + shift) % array.shape[longest]
        spots.append(tuple(where))
    return array.at[spots[0]].set(low).at[spots[1]].set(top_value)


def block_levels(rng, extent, split, smallest, largest):
    level = 1.0
    for position, blocks in split:
        draws = jax.random.uniform(jax.random.fold_in(jax.random.fold_in(rng, 6), position), (blocks,), jnp.float32, smallest / len(split), largest / len(split))
        level = level * jnp.repeat(jnp.exp(draws), extent[position] // blocks).reshape((-1,) + (1,) * (len(extent) - 1 - position))
    return level


def gaussian(own_key, dims, scale, limit, cuts=(), dtype=jnp.bfloat16):
    array = jax.random.normal(own_key, dims, jnp.float32) * scale
    if len(cuts) > 0:
        array = block_levels(own_key, dims, cuts, -0.22, 0.18) * array
    return jnp.clip(array, min=-limit, max=limit).astype(dtype)


def setup_inputs(seed: int = 0) -> dict:
    arg_keys = jax.random.split(jax.random.key(seed), 7)
    initial = gaussian(arg_keys[0], (3, NY, NX), 1.0, 6.0, ((1, 32),), jnp.float32)
    guess = gaussian(arg_keys[1], (INTERVALS, 3, NY, NX), 1.0, 6.0, ((0, 4), (2, 32)), jnp.float32)
    depth = jnp.clip(0.2 + 0.8 * jax.random.uniform(arg_keys[2], (NY, NX), jnp.float32) ** block_levels(arg_keys[2], (NY, NX), ((0, 32),), -0.2, 0.2), 0.2, 1.0)
    friction = jnp.clip(jnp.exp(math.log(0.1) - 2.9957323 * jax.random.uniform(arg_keys[3], (NY, NX), jnp.float32) ** block_levels(arg_keys[3], (NY, NX), ((0, 32),), -0.2, 0.2)), 0.005, 0.1)
    mask = with_ends((jax.random.randint(arg_keys[4], (NY, NX), 0, 8) < 7).astype(jnp.int32), jax.random.fold_in(arg_keys[4], 1), 0, 1)
    wind = gaussian(arg_keys[5], (INTERVALS, 2, NY, NX), 1.0, 6.0, ((0, 4), (2, 32)), jnp.float32)
    return dict(initial=initial, guess=guess, depth=depth, friction=friction, mask=mask, wind=wind)


delta_fine = 0.05


def diff_x(field):
    padded = jnp.pad(field, [(0, 0)] * (field.ndim - 1) + [(1, 1)])
    return (padded[..., 2:] - padded[..., :-2]) * 0.5


def diff_y(field):
    padded = jnp.pad(field, [(1, 1), (0, 0)])
    return (padded[2:] - padded[:-2]) * 0.5


def one_step(state, delta, forcing, depth, friction, maskf):
    level = state[0] - delta * (diff_x(depth * state[1]) + diff_y(depth * state[2]))
    damping = 1.0 + delta * friction
    u_new = maskf * (state[1] - delta * diff_x(level) + delta * forcing[0]) / damping
    v_new = maskf * (state[2] - delta * diff_y(level) + delta * forcing[1]) / damping
    return jnp.stack([level, u_new, v_new])


def reference(initial, guess, depth, friction, mask, wind):
    maskf = mask.astype(jnp.float32)

    def sweep(pair):
        start, forcing = pair
        return lax.fori_loop(0, FACTOR, lambda i, s: one_step(s, delta_fine, forcing, depth, friction, maskf), start)

    starts = jnp.concatenate([initial[None], guess[:-1]], axis=0)
    first = lax.map(sweep, (starts, wind))
    starts = jnp.concatenate([initial[None], first[:-1]], axis=0)
    second = lax.map(sweep, (starts, wind))
    resid = second - first
    zero_force = jnp.zeros((2,) + depth.shape, jnp.float32)

    def link(carried, term):
        new = one_step(carried, delta_fine * FACTOR, zero_force, depth, friction, maskf) + term
        return new, new

    _, errors = lax.scan(link, jnp.zeros_like(initial), resid)
    return first + errors
```

```python
import jax
import jax.numpy as jnp
from jax import lax
from jax.experimental import pallas as pl
from jax.experimental.pallas import tpu as pltpu
from jax.sharding import PartitionSpec as P

FACTOR = 16
H = 0.05
C = 0.5 * H
CHUNK = 8
PAD = 16


def ring(n, shift):
    return [(i, (i + shift) % n) for i in range(n)]


def lane_masks():
    lane = lax.broadcasted_iota(jnp.int32, (8, 128), 1)
    sub = lax.broadcasted_iota(jnp.int32, (8, 128), 0)
    return (
        lane == 0,
        lane == 127,
        (lane == 0) & (sub == 0),
        (lane == 127) & (sub == 7),
    )


def diff_cols(f, masks):
    first, last, corner_lo, corner_hi = masks
    left = pltpu.roll(f, 1, 1)
    right = pltpu.roll(f, 127, 1)
    left = jnp.where(first, pltpu.roll(left, 1, 0), left)
    right = jnp.where(last, pltpu.roll(right, 7, 0), right)
    left = jnp.where(corner_lo, 0.0, left)
    right = jnp.where(corner_hi, 0.0, right)
    return right - left


def row_at(ref, r):
    return ref[pl.ds(pl.multiple_of(r * 8, 8), 8), :]


def put_row(ref, r, value):
    ref[pl.ds(pl.multiple_of(r * 8, 8), 8), :] = value


def spread(dst, base, src, lead, rows, scale=None, start=0):
    def group(g, _):
        for j in range(8):
            val = src[lead + (pl.ds(pl.multiple_of(start + g * 8, 8), 8), pl.ds(j * 128, 128))]
            if scale is not None:
                val = val * scale
            dst[pl.ds((base + g * 8) * 8 + j, 8, stride=8), :] = val
        return 0

    lax.fori_loop(0, rows // 8, group, 0)


def gather_rows(src, base, g, j):
    return src[pl.ds((base + g * 8) * 8 + j, 8, stride=8), :]


def one_step(E, U, V, D, A, W, lo, n, top, bottom, gain, masks, write=None):
    chunks = (n + CHUNK - 1) // CHUNK

    def flux_y(r):
        return row_at(D, r) * row_at(V, r)

    def level(r, above, below):
        flux = diff_cols(row_at(D, r) * row_at(U, r), masks) + (below - above)
        if gain != 1.0:
            flux = flux * gain
        keep = jnp.where((r == top) | (r == bottom), 0.0, 1.0)
        return (row_at(E, r) - flux) * keep

    f0, f1, f2, f3 = (flux_y(lo + k) for k in (-2, -1, 0, 1))
    before = level(lo - 1, f0, f2)
    here = level(lo, f1, f3)
    put_row(E, lo, here)

    def body(k, carry):
        fa, fb, ea, eb = carry
        r = lo + k * CHUNK
        for i in range(CHUNK):
            fc = flux_y(r + i + 2)
            ec = level(r + i + 1, fa, fc)
            a = row_at(A, r + i)
            gx = diff_cols(eb, masks)
            gy = ec - ea
            if gain != 1.0:
                gx, gy = gx * gain, gy * gain
            un = a * (row_at(U, r + i) - gx)
            vn = a * (row_at(V, r + i) - gy)
            if W is not None:
                un = un + row_at(W[0], r + i)
                vn = vn + row_at(W[1], r + i)
            put_row(E, r + i + 1, ec)
            put_row(U, r + i, un)
            put_row(V, r + i, vn)
            fa, fb, ea, eb = fb, fc, eb, ec
        return fa, fb, ea, eb

    lax.fori_loop(0, chunks, body, (f2, f3, before, here))


def sweep_steps(E, U, V, D, A, W, lo0, rows0, top, bottom, masks):
    def step(s, _):
        one_step(E, U, V, D, A, W, lo0 + 2 * s, rows0 - 4 * s, top, bottom, 1.0, masks)
        return 0

    lax.fori_loop(1, FACTOR + 1, step, 0)


def edge_rows(space, top_row, bottom_row):
    size = lax.axis_size("space")
    return jnp.where(space == 0, top_row, -1), jnp.where(space == size - 1, bottom_row, -1)


def fine_kernel(n, space_ref, own, up, dn, wind, wup, wdn, coef, cup, cdn, nxt, first, delta, E, U, V, D, A, W0, W1):
    masks = lane_masks()
    space = space_ref[0]
    top, bottom = edge_rows(space, n - 1, 2 * n)
    in_up = jnp.where(space == 0, 0.0, 1.0)
    in_dn = jnp.where(space == lax.axis_size("space") - 1, 0.0, 1.0)
    for base, st, wd, cf, inside in ((0, up, wup, cup, in_up), (n, own, wind, coef, 1.0), (2 * n, dn, wdn, cdn, in_dn)):
        spread(D, base, cf, (0,), n, inside * (C * C))
        spread(A, base, cf, (1,), n, inside)
        spread(E, base, st, (0,), n, C)
        spread(U, base, st, (1,), n)
        spread(V, base, st, (2,), n)
        spread(W0, base, wd, (0,), n, H)
        spread(W1, base, wd, (1,), n, H)

    def force(r, _):
        a = row_at(A, r)
        put_row(W0, r, a * row_at(W0, r))
        put_row(W1, r, a * row_at(W1, r))
        return 0

    lax.fori_loop(0, 3 * n, force, 0)
    sweep_steps(E, U, V, D, A, (W0, W1), 0, 3 * n, top, bottom, masks)

    def out(g, _):
        rows = pl.ds(pl.multiple_of(g * 8, 8), 8)
        for f, src in enumerate((E, U, V)):
            for j in range(8):
                cols = pl.ds(j * 128, 128)
                val = gather_rows(src, n, g, j)
                if f == 0:
                    val = val * (1.0 / C)
                first[f, rows, cols] = val
                delta[f, rows, cols] = val - nxt[f, rows, cols]
        return 0

    lax.fori_loop(0, n // 8, out, 0)


def relax_kernel(n, space_ref, d1, d1u, d1d, d1uu, d1dd, d2, d2u, d2d, coef, cup, cdn, cuu, cdd, r1, c1, E, U, V, D, A, E2, U2, V2):
    masks = lane_masks()
    space = space_ref[0]
    off = n + 8
    size = lax.axis_size("space")
    top, bottom = edge_rows(space, off - 1, off + n)
    in_up = jnp.where(space == 0, 0.0, 1.0)
    in_dn = jnp.where(space == size - 1, 0.0, 1.0)
    in_uu = jnp.where(space <= 1, 0.0, 1.0)
    in_dd = jnp.where(space >= size - 2, 0.0, 1.0)
    for base, rows, cf, inside in ((0, 8, cuu, in_uu), (8, n, cup, in_up), (off, n, coef, 1.0), (off + n, n, cdn, in_dn), (off + 2 * n, 8, cdd, in_dd)):
        spread(D, base, cf, (0,), rows, inside * (C * C))
        spread(A, base, cf, (1,), rows, inside)
    for base, rows, st in ((0, 8, d1uu), (8, n, d1u), (off, n, d1), (off + n, n, d1d), (off + 2 * n, 8, d1dd)):
        spread(E, base, st, (0,), rows, C)
        spread(U, base, st, (1,), rows)
        spread(V, base, st, (2,), rows)
    for base, st in ((8, d2u), (off, d2), (off + n, d2d)):
        spread(E2, base, st, (0,), n, C)
        spread(U2, base, st, (1,), n)
        spread(V2, base, st, (2,), n)
    sweep_steps(E2, U2, V2, D, A, None, 8, 3 * n, top, bottom, masks)
    sweep_steps(E, U, V, D, A, None, 6, 3 * n + 4, top, bottom, masks)

    def out_r(g, _):
        rows = pl.ds(pl.multiple_of(g * 8, 8), 8)
        for f, src in enumerate((E, U, V)):
            for j in range(8):
                cols = pl.ds(j * 128, 128)
                r1[f, rows, cols] = gather_rows(src, off, g, j)
        return 0

    lax.fori_loop(0, n // 8, out_r, 0)

    def coarse_coef(r, _):
        a = row_at(A, off - 2 + r)
        put_row(A, off - 2 + r, a / (float(FACTOR) - (FACTOR - 1.0) * a))
        return 0

    lax.fori_loop(0, n + 4, coarse_coef, 0)
    one_step(E, U, V, D, A, None, off, n, top, bottom, float(FACTOR), masks)

    def out_c(g, _):
        rows = pl.ds(pl.multiple_of(g * 8, 8), 8)
        for f, (src, more) in enumerate(((E, E2), (U, U2), (V, V2))):
            for j in range(8):
                cols = pl.ds(j * 128, 128)
                c1[f, rows, cols] = gather_rows(src, off, g, j) + gather_rows(more, off, g, j)
        return 0

    lax.fori_loop(0, n // 8, out_c, 0)


HALO = 16


def chain_kernel(n, pos_ref, ca, cau, cad, cb, cbu, cbd, cc, ccu, ccd, coef, cup, cdn, r1, fa, fb, out, E, U, V, D, A, X, Y, Z):
    masks = lane_masks()
    tm, space = pos_ref[0], pos_ref[1]
    off = HALO
    top, bottom = edge_rows(space, off - 1, off + n)
    in_up = jnp.where(space == 0, 0.0, 1.0)
    in_dn = jnp.where(space == lax.axis_size("space") - 1, 0.0, 1.0)
    spread(D, 0, cup, (0,), HALO, in_up * (C * C), start=n - HALO)
    spread(A, 0, cup, (1,), HALO, in_up, start=n - HALO)
    spread(D, off, coef, (0,), n, C * C)
    spread(A, off, coef, (1,), n)
    spread(D, off + n, cdn, (0,), HALO, in_dn * (C * C))
    spread(A, off + n, cdn, (1,), HALO, in_dn)

    def coarse_coef(r, _):
        a = row_at(A, r)
        put_row(A, r, a / (float(FACTOR) - (FACTOR - 1.0) * a))
        return 0

    lax.fori_loop(0, n + 2 * HALO, coarse_coef, 0)

    def take(dst, f, own, u, d, use):
        spread(dst, 0, u, (f,), HALO, use)
        spread(dst, off, own, (f,), n, use)
        spread(dst, off + n, d, (f,), HALO, use)

    for f, dst in enumerate((E, U, V)):
        take(dst, f, cc, ccu, ccd, jnp.where(tm >= 3, 1.0, 0.0))

    def coarse(lo, rows):
        one_step(E, U, V, D, A, None, lo, rows, top, bottom, float(FACTOR), masks)

    def add(lo, rows):
        def body(r, _):
            for dst, src in ((E, X), (U, Y), (V, Z)):
                put_row(dst, lo + r, row_at(dst, lo + r) + row_at(src, lo + r))
            return 0

        lax.fori_loop(0, rows, body, 0)

    coarse(off - 8, n + 16)
    coarse(off - 6, n + 12)
    for f, dst in enumerate((X, Y, Z)):
        take(dst, f, cb, cbu, cbd, jnp.where(tm >= 2, 1.0, 0.0))
    add(off - 6, n + 12)
    coarse(off - 4, n + 8)
    coarse(off - 2, n + 4)
    for f, dst in enumerate((X, Y, Z)):
        take(dst, f, ca, cau, cad, jnp.where(tm >= 1, 1.0, 0.0))
    add(off - 2, n + 4)

    def write(k, first, more):
        def group(g, _):
            rows = pl.ds(pl.multiple_of(g * 8, 8), 8)
            for f, src in enumerate((E, U, V)):
                for j in range(8):
                    cols = pl.ds(j * 128, 128)
                    val = gather_rows(src, off, g, j)
                    if more is not None:
                        val = val + more[f, rows, cols]
                    if f == 0:
                        val = val * (1.0 / C)
                    out[k, f, rows, cols] = first[f, rows, cols] + val
            return 0

        lax.fori_loop(0, n // 8, group, 0)

    write(0, fa, None)
    coarse(off, n)
    write(1, fb, r1)


def call(kernel, n, rows, fields, outs, *args):
    scratch = [pltpu.VMEM(((rows + PAD) * 8, 128), jnp.float32)] * fields
    vmem = pl.BlockSpec(memory_space=pltpu.VMEM)
    return pl.pallas_call(
        lambda *refs: kernel(n, *refs),
        out_shape=outs,
        in_specs=[pl.BlockSpec(memory_space=pltpu.SMEM)] + [vmem] * (len(args) - 1),
        out_specs=jax.tree.map(lambda _: vmem, outs),
        scratch_shapes=scratch,
        compiler_params=pltpu.CompilerParams(vmem_limit_bytes=32 * 2**20),
    )(*args)


def shards(initial, guess, depth, friction, mask, wind):
    n, ncols = depth.shape
    spaces, times = lax.axis_size("space"), lax.axis_size("tm")
    tm, space = lax.axis_index("tm"), lax.axis_index("space")
    pos = jnp.stack([tm, space]).astype(jnp.int32)
    where = space.astype(jnp.int32)[None]

    def sides(x, hop=1):
        return lax.ppermute(x, "space", ring(spaces, hop)), lax.ppermute(x, "space", ring(spaces, -hop))

    def ends(x, rows, hop=1):
        up = lax.ppermute(x[:, n - rows :], "space", ring(spaces, hop))
        dn = lax.ppermute(x[:, :rows], "space", ring(spaces, -hop))
        return up, dn

    state = jax.ShapeDtypeStruct((3, n, ncols), jnp.float32)
    coef = jnp.stack([depth, mask.astype(jnp.float32) / (1.0 + H * friction)])

    earlier = lax.ppermute(guess[1], "tm", ring(times, 1))
    pack_b = jnp.concatenate([guess[0], wind[1], coef])
    bu, bd = sides(pack_b)
    entry = jnp.where(tm == 0, initial, earlier)
    pack_a = jnp.concatenate([entry, wind[0]])
    au, ad = sides(pack_a)
    cuu, cdd = ends(coef, 8, 2)

    fb, db = call(fine_kernel, n, 3 * n, 7, (state, state), where, guess[0], bu[:3], bd[:3], wind[1], bu[3:5], bd[3:5], coef, bu[5:], bd[5:], guess[1])
    dbu, dbd = sides(db)
    fa, da = call(fine_kernel, n, 3 * n, 7, (state, state), where, entry, au[:3], ad[:3], wind[0], au[3:], ad[3:], coef, bu[5:], bd[5:], guess[0])
    dau, dad = sides(da)
    dauu, dadd = ends(da, 8, 2)
    r1, c1 = call(relax_kernel, n, 3 * n + 16, 8, (state, state), where, da, dau, dad, dauu, dadd, db, dbu, dbd, coef, bu[5:], bd[5:], cuu, cdd)

    ca = lax.ppermute(c1, "tm", ring(times, 1))
    cc = lax.ppermute(c1, "tm", ring(times, -1))
    half = n // 2
    cb = jnp.concatenate(
        [lax.ppermute(ca[:, :half], "tm", ring(times, 1)), lax.ppermute(cc[:, half:], "tm", ring(times, -1))], axis=1
    )
    rim = jnp.stack([ca[:, -HALO:], cb[:, -HALO:], cc[:, -HALO:]])
    rim_up = lax.ppermute(rim, "space", ring(spaces, 1))
    rim = jnp.stack([ca[:, :HALO], cb[:, :HALO], cc[:, :HALO]])
    rim_dn = lax.ppermute(rim, "space", ring(spaces, -1))
    out = jax.ShapeDtypeStruct(guess.shape, jnp.float32)
    return call(
        chain_kernel, n, n + 2 * HALO, 8, out, pos, ca, rim_up[0], rim_dn[0], cb, rim_up[1], rim_dn[1], cc, rim_up[2], rim_dn[2],
        coef, bu[5:], bd[5:], r1, fa, fb,
    )


def solution(mesh):
    return jax.shard_map(
        shards,
        mesh=mesh,
        in_specs=(
            P(None, "space", None),
            P("tm", None, "space", None),
            P("space", None),
            P("space", None),
            P("space", None),
            P("tm", None, "space", None),
        ),
        out_specs=P("tm", None, "space", None),
        check_vma=False,
    )
```

```python
import functools

import jax
import jax.numpy as jnp
from jax import lax
from jax.experimental import pallas as pl
from jax.experimental.pallas import tpu as pltpu
from jax.sharding import PartitionSpec as P

FACTOR = 16
H = 0.05
C = 0.5 * H
LANES = 128


def ring(n, shift):
    return [(i, (i + shift) % n) for i in range(n)]


def at(r, rows=8):
    return pl.ds(r, rows)


def diff_cols(chunks):
    lane = lax.broadcasted_iota(jnp.int32, (8, LANES), 1)
    first, last = lane == 0, lane == LANES - 1
    left = [pltpu.roll(f, 1, 1) for f in chunks]
    right = [pltpu.roll(f, LANES - 1, 1) for f in chunks]
    out = []
    for c in range(len(chunks)):
        lo = jnp.where(first, left[c - 1] if c > 0 else 0.0, left[c])
        hi = jnp.where(last, right[c + 1] if c + 1 < len(chunks) else 0.0, right[c])
        out.append(hi - lo)
    return out


def copy_in(dst, base, src, lead, start, rows, scale=None):
    for g in range(0, rows, 8):
        for c in range(dst.shape[0]):
            val = src[lead + (at(start + g), pl.ds(c * LANES, LANES))]
            dst[c, at(base + g), :] = val if scale is None else val * scale


def each(fields, base, rows, f):
    def group(g, _):
        for c in range(fields[0].shape[0]):
            f((c, at(base + g * 8), slice(None)))
        return 0

    lax.fori_loop(0, rows // 8, group, 0)


def flux_rows(FY, V, D, base, rows):
    def put(s):
        FY[s] = D[s] * V[s]

    each((FY,), base, rows, put)


def level_pass(E, U, FY, D, r):
    cs = range(E.shape[0])
    dx = diff_cols([D[c, at(r), :] * U[c, at(r), :] for c in cs])
    for c in cs:
        E[c, at(r), :] = E[c, at(r), :] - (dx[c] + (FY[c, at(r + 1), :] - FY[c, at(r - 1), :]))


def velocity_pass(E, U, V, FY, D, A, W, r, gain=None):
    cs = range(E.shape[0])
    dx = diff_cols([E[c, at(r), :] for c in cs])
    for c in cs:
        s = (c, at(r), slice(None))
        dy = E[c, at(r + 1), :] - E[c, at(r - 1), :]
        gx = dx[c]
        if gain is not None:
            gx, dy = gx * gain, dy * gain
        u = A[s] * (U[s] - gx)
        v = A[s] * (V[s] - dy)
        if W is not None:
            u, v = u + W[0][s], v + W[1][s]
        U[s] = u
        V[s] = v
        FY[s] = D[s] * v


def keep_rim(E, base, n, keep):
    for r, k in ((base - 1, keep[0]), (base + n, keep[1])):
        for c in range(E.shape[0]):
            E[c, at(r, 1), :] = E[c, at(r, 1), :] * k


def sweep(E, U, V, FY, D, A, W, base, n, keep, wide):
    for phase in range(FACTOR // 4):
        reach = 2 * FACTOR - 8 * phase
        lo, groups = base - reach, (n + 2 * reach) // 8

        def step(_, carry, lo=lo, groups=groups):
            for g in range(groups + wide):
                level_pass(E, U, FY, D, lo - wide + g * 8)
            keep_rim(E, base, n, keep)
            for g in range(groups):
                velocity_pass(E, U, V, FY, D, A, W, lo + g * 8)
            return carry

        lax.fori_loop(0, 4, step, 0)


def coarse_coefs(D, A, base, rows):
    def put(s):
        D[s] = D[s] * float(FACTOR)
        A[s] = A[s] / (float(FACTOR) - (FACTOR - 1.0) * A[s])

    each((D, A), base, rows, put)


def coarse_step(E, U, V, FY, D, A, lo, rows, base, n, keep):
    for r in range(lo - 1, lo + rows + 1, 8):
        level_pass(E, U, FY, D, r)
    keep_rim(E, base, n, keep)
    for r in range(lo, lo + rows, 8):
        velocity_pass(E, U, V, FY, D, A, None, r, float(FACTOR))


def rim_flags(space):
    size = lax.axis_size("space")
    return tuple(jnp.where(x, 1.0, 0.0) for x in (space > 0, space < size - 1, space > 1, space < size - 2))


def read_own(src, base, g, c):
    return src[c, at(base + g), :]


def fine_kernel(k, pack, n, space_ref, own, up, dn, wind, wup, wdn, coef, cup, cdn, guess, first, delta, E, U, V, FY, D, A, W0, W1):
    in_up, in_dn, _, _ = rim_flags(space_ref[0])
    lead, ws, cs = pack
    base = 40
    parts = ((base - n, up, wup, cup, in_up, (), ws, cs), (base, own, wind, coef, 1.0, lead, None, 0), (base + n, dn, wdn, cdn, in_dn, (), ws, cs))
    for row, st, wd, cf, inside, ld, w, c in parts:
        copy_in(D, row, cf, (c,), 0, n, inside * (C * C))
        copy_in(A, row, cf, (c + 1,), 0, n, inside)
        copy_in(E, row, st, ld + (0,), 0, n, C)
        copy_in(U, row, st, ld + (1,), 0, n)
        copy_in(V, row, st, ld + (2,), 0, n)
        for f, dst in enumerate((W0, W1)):
            copy_in(dst, row, wd, (k, f) if w is None else (w + f,), 0, n, H)

    def prepare(s):
        W0[s] = W0[s] * A[s]
        W1[s] = W1[s] * A[s]
        FY[s] = D[s] * V[s]

    each((E,), base - n, 3 * n, prepare)
    sweep(E, U, V, FY, D, A, (W0, W1), base, n, (in_up, in_dn), 0)
    for f, src in enumerate((E, U, V)):
        for g in range(0, n, 8):
            for c in range(E.shape[0]):
                to = (f, at(g), pl.ds(c * LANES, LANES))
                val = read_own(src, base, g, c)
                if f == 0:
                    val = val * (1.0 / C)
                first[to] = val
                delta[to] = val - guess[(k,) + to]


def relax_b_kernel(n, space_ref, d, up, dn, coef, cup, cdn, res, E, U, V, FY, D, A):
    in_up, in_dn, _, _ = rim_flags(space_ref[0])
    base = 40
    for row, st, cf, inside, c in ((base - n, up, cup, in_up, 5), (base, d, coef, 1.0, 0), (base + n, dn, cdn, in_dn, 5)):
        copy_in(D, row, cf, (c,), 0, n, inside * (C * C))
        copy_in(A, row, cf, (c + 1,), 0, n, inside)
        copy_in(E, row, st, (0,), 0, n, C)
        copy_in(U, row, st, (1,), 0, n)
        copy_in(V, row, st, (2,), 0, n)
    flux_rows(FY, V, D, base - n, 3 * n)
    sweep(E, U, V, FY, D, A, None, base, n, (in_up, in_dn), 0)
    for f, src in enumerate((E, U, V)):
        for g in range(0, n, 8):
            for c in range(E.shape[0]):
                res[f, at(g), pl.ds(c * LANES, LANES)] = read_own(src, base, g, c)


def relax_a_kernel(n, space_ref, d, up, dn, uup, ddn, coef, cup, cdn, cuu, cdd, more, res, total, E, U, V, FY, D, A):
    in_up, in_dn, in_uu, in_dd = rim_flags(space_ref[0])
    base = 48
    for row, rows, st, cf, inside, c in (
        (base - n - 8, 8, uup, cuu, in_uu, 0),
        (base - n, n, up, cup, in_up, 5),
        (base, n, d, coef, 1.0, 0),
        (base + n, n, dn, cdn, in_dn, 5),
        (base + 2 * n, 8, ddn, cdd, in_dd, 0),
    ):
        copy_in(D, row, cf, (c,), 0, rows, inside * (C * C))
        copy_in(A, row, cf, (c + 1,), 0, rows, inside)
        copy_in(E, row, st, (0,), 0, rows, C)
        copy_in(U, row, st, (1,), 0, rows)
        copy_in(V, row, st, (2,), 0, rows)
    flux_rows(FY, V, D, base - n - 8, 3 * n + 16)
    sweep(E, U, V, FY, D, A, None, base, n, (in_up, in_dn), 1)
    for f, src in enumerate((E, U, V)):
        for g in range(0, n, 8):
            for c in range(E.shape[0]):
                res[f, at(g), pl.ds(c * LANES, LANES)] = read_own(src, base, g, c)
    coarse_coefs(D, A, base - 8, n + 16)
    flux_rows(FY, V, D, base - 8, n + 16)
    coarse_step(E, U, V, FY, D, A, base, n, base, n, (in_up, in_dn))
    for f, src in enumerate((E, U, V)):
        for g in range(0, n, 8):
            for c in range(E.shape[0]):
                to = (f, at(g), pl.ds(c * LANES, LANES))
                total[to] = read_own(src, base, g, c) + more[to]


HALO = 16


def chain_kernel(n, pos_ref, ca, cb, cc, rup, rdn, coef, cup, cdn, r1, fa, fb, out, E, U, V, FY, D, A, X, Y, Z):
    tm, space = pos_ref[0], pos_ref[1]
    base = HALO + 8
    in_up, in_dn, _, _ = rim_flags(space)
    keep = (in_up, in_dn)
    for row, cf, c, start, rows, inside in (
        (base - HALO, cup, 5, n - HALO, HALO, in_up),
        (base, coef, 0, 0, n, 1.0),
        (base + n, cdn, 5, 0, HALO, in_dn),
    ):
        copy_in(D, row, cf, (c,), start, rows, inside * (C * C))
        copy_in(A, row, cf, (c + 1,), start, rows, inside)
    coarse_coefs(D, A, base - HALO, n + 2 * HALO)

    def take(fields, k, own, use):
        for f, dst in enumerate(fields):
            copy_in(dst, base - HALO, rup, (k, f), 0, HALO, use)
            copy_in(dst, base, own, (f,), 0, n, use)
            copy_in(dst, base + n, rdn, (k, f), 0, HALO, use)

    def add(lo, rows):
        def put(s):
            E[s] = E[s] + X[s]
            U[s] = U[s] + Y[s]
            V[s] = V[s] + Z[s]
            FY[s] = D[s] * V[s]

        each((E,), lo, rows, put)

    def coarse(reach):
        coarse_step(E, U, V, FY, D, A, base - reach, n + 2 * reach, base, n, keep)

    take((E, U, V), 2, cc, jnp.where(tm >= 3, 1.0, 0.0))
    flux_rows(FY, V, D, base - HALO, n + 2 * HALO)
    coarse(8)
    coarse(6)
    take((X, Y, Z), 1, cb, jnp.where(tm >= 2, 1.0, 0.0))
    add(base - 8, n + 16)
    coarse(4)
    coarse(2)
    take((X, Y, Z), 0, ca, jnp.where(tm >= 1, 1.0, 0.0))
    add(base - 8, n + 16)

    def write(k, first, more):
        for f, src in enumerate((E, U, V)):
            for g in range(0, n, 8):
                for c in range(E.shape[0]):
                    to = (f, at(g), pl.ds(c * LANES, LANES))
                    val = read_own(src, base, g, c)
                    if more is not None:
                        val = val + more[to]
                    if f == 0:
                        val = val * (1.0 / C)
                    out[(k,) + to] = first[to] + val

    write(0, fa, None)
    coarse(0)
    write(1, fb, r1)


def call(kernel, n, ncols, rows, fields, outs, *args):
    scratch = [pltpu.VMEM((ncols // LANES, rows, LANES), jnp.float32)] * fields
    vmem = pl.BlockSpec(memory_space=pltpu.VMEM)
    return pl.pallas_call(
        lambda *refs: kernel(n, *refs),
        out_shape=outs,
        in_specs=[pl.BlockSpec(memory_space=pltpu.SMEM)] + [vmem] * (len(args) - 1),
        out_specs=jax.tree.map(lambda _: vmem, outs),
        scratch_shapes=scratch,
        compiler_params=pltpu.CompilerParams(vmem_limit_bytes=32 * 2**20),
    )(*args)


def shards(initial, guess, depth, friction, mask, wind):
    n, ncols = depth.shape
    spaces, times = lax.axis_size("space"), lax.axis_size("tm")
    tm, space = lax.axis_index("tm"), lax.axis_index("space")
    pos = jnp.stack([tm, space]).astype(jnp.int32)
    where = space.astype(jnp.int32)[None]

    def sides(x, hop=1):
        return lax.ppermute(x, "space", ring(spaces, hop)), lax.ppermute(x, "space", ring(spaces, -hop))

    def ends(x, rows, hop=1):
        up = lax.ppermute(x[..., n - rows :, :], "space", ring(spaces, hop))
        dn = lax.ppermute(x[..., :rows, :], "space", ring(spaces, -hop))
        return up, dn

    state = jax.ShapeDtypeStruct((3, n, ncols), jnp.float32)
    coef = jnp.stack([depth, mask.astype(jnp.float32) / (1.0 + H * friction)])

    earlier = lax.ppermute(guess[1], "tm", ring(times, 1))
    bu, bd = sides(jnp.concatenate([guess[0], wind[1], coef]))
    entry = jnp.where(tm == 0, initial, earlier)
    au, ad = sides(jnp.concatenate([entry, wind[0]]))
    cuu, cdd = ends(coef, 8, 2)

    fine_b = functools.partial(fine_kernel, 1, ((0,), 3, 5))
    fb, db = call(fine_b, n, ncols, 120, 8, (state, state), where, guess, bu, bd, wind, bu, bd, coef, bu, bd, guess)
    dbu, dbd = sides(db)
    fine_a = functools.partial(fine_kernel, 0, ((), 3, 5))
    fa, da = call(fine_a, n, ncols, 120, 8, (state, state), where, entry, au, ad, wind, au, ad, coef, bu, bd, guess)
    dau, dad = sides(da)
    dauu, dadd = ends(da, 8, 2)
    rb = call(relax_b_kernel, n, ncols, 120, 6, state, where, db, dbu, dbd, coef, bu, bd)
    ra, c1 = call(relax_a_kernel, n, ncols, 144, 6, (state, state), where, da, dau, dad, dauu, dadd, coef, bu, bd, cuu, cdd, rb)

    ca = lax.ppermute(c1, "tm", ring(times, 1))
    cc = lax.ppermute(c1, "tm", ring(times, -1))
    half = n // 2
    cb = jnp.concatenate(
        [lax.ppermute(ca[:, :half], "tm", ring(times, 1)), lax.ppermute(cc[:, half:], "tm", ring(times, -1))], axis=1
    )
    rup, rdn = ends(jnp.stack([ca, cb, cc]), HALO)
    out = jax.ShapeDtypeStruct(guess.shape, jnp.float32)
    return call(chain_kernel, n, ncols, 88, 9, out, pos, ca, cb, cc, rup, rdn, coef, bu, bd, ra, fa, fb)


def solution(mesh):
    return jax.shard_map(
        shards,
        mesh=mesh,
        in_specs=(
            P(None, "space", None),
            P("tm", None, "space", None),
            P("space", None),
            P("space", None),
            P("space", None),
            P("tm", None, "space", None),
        ),
        out_specs=P("tm", None, "space", None),
        check_vma=False,
    )
```

```python
import functools

import jax
import jax.numpy as jnp
from jax import lax
from jax.experimental import pallas as pl
from jax.experimental.pallas import tpu as pltpu
from jax.sharding import PartitionSpec as P

FACTOR = 16
H = 0.05
C = 0.5 * H
LANES = 128


def ring(n, shift):
    return [(i, (i + shift) % n) for i in range(n)]


def at(r, rows=8):
    return pl.ds(r, rows)


def diff_cols(chunks):
    lane = lax.broadcasted_iota(jnp.int32, (8, LANES), 1)
    first, last = lane == 0, lane == LANES - 1
    left = [pltpu.roll(f, 1, 1) for f in chunks]
    right = [pltpu.roll(f, LANES - 1, 1) for f in chunks]
    out = []
    for c in range(len(chunks)):
        lo = jnp.where(first, left[c - 1] if c > 0 else 0.0, left[c])
        hi = jnp.where(last, right[c + 1] if c + 1 < len(chunks) else 0.0, right[c])
        out.append(hi - lo)
    return out


def copy_in(dst, base, src, lead, start, rows, scale=None):
    for g in range(0, rows, 8):
        count = min(8, rows - g)
        for c in range(dst.shape[0]):
            val = src[lead + (at(start + g, count), pl.ds(c * LANES, LANES))]
            dst[c, at(base + g, count), :] = val if scale is None else val * scale


def each(fields, base, rows, f):
    def group(g, _):
        for c in range(fields[0].shape[0]):
            f((c, at(base + g * 8), slice(None)))
        return 0

    lax.fori_loop(0, rows // 8, group, 0)


def flux_rows(FY, V, D, base, rows):
    def put(s):
        FY[s] = D[s] * V[s]

    each((FY,), base, rows, put)


def level_pass(E, U, FY, D, r):
    cs = range(E.shape[0])
    dx = diff_cols([D[c, at(r), :] * U[c, at(r), :] for c in cs])
    for c in cs:
        E[c, at(r), :] = E[c, at(r), :] - (dx[c] + (FY[c, at(r + 1), :] - FY[c, at(r - 1), :]))


def velocity_pass(E, U, V, FY, D, A, W, r, gain=None):
    cs = range(E.shape[0])
    dx = diff_cols([E[c, at(r), :] for c in cs])
    for c in cs:
        s = (c, at(r), slice(None))
        dy = E[c, at(r + 1), :] - E[c, at(r - 1), :]
        gx = dx[c]
        if gain is not None:
            gx, dy = gx * gain, dy * gain
        u = A[s] * (U[s] - gx)
        v = A[s] * (V[s] - dy)
        if W is not None:
            u, v = u + W[0][s], v + W[1][s]
        U[s] = u
        V[s] = v
        FY[s] = D[s] * v


def keep_rim(E, base, n, keep):
    for r, k in ((base - 1, keep[0]), (base + n, keep[1])):
        for c in range(E.shape[0]):
            E[c, at(r, 1), :] = E[c, at(r, 1), :] * k


def sweep(E, U, V, FY, D, A, W, base, n, keep, wide):
    for phase in range(FACTOR // 4):
        reach = 2 * FACTOR - 8 * phase
        lo, groups = base - reach, (n + 2 * reach) // 8

        def step(_, carry, lo=lo, groups=groups):
            for g in range(groups + wide):
                level_pass(E, U, FY, D, lo - wide + g * 8)
            keep_rim(E, base, n, keep)
            for g in range(groups):
                velocity_pass(E, U, V, FY, D, A, W, lo + g * 8)
            return carry

        lax.fori_loop(0, 4, step, 0)


def coarse_coefs(D, A, base, rows):
    def put(s):
        D[s] = D[s] * float(FACTOR)
        A[s] = A[s] / (float(FACTOR) - (FACTOR - 1.0) * A[s])

    each((D, A), base, rows, put)


def coarse_step(E, U, V, FY, D, A, lo, rows, base, n, keep):
    for r in range(lo - 1, lo + rows + 1, 8):
        level_pass(E, U, FY, D, r)
    keep_rim(E, base, n, keep)
    for r in range(lo, lo + rows, 8):
        velocity_pass(E, U, V, FY, D, A, None, r, float(FACTOR))


def rim_flags(space):
    size = lax.axis_size("space")
    return tuple(jnp.where(x, 1.0, 0.0) for x in (space > 0, space < size - 1, space > 1, space < size - 2))


def read_own(src, base, g, c):
    return src[c, at(base + g), :]


def fine_kernel(k, pack, n, space_ref, own, up, dn, wind, wup, wdn, coef, cup, cdn, guess, first, delta, E, U, V, FY, D, A, W0, W1):
    in_up, in_dn, _, _ = rim_flags(space_ref[0])
    lead, ws, cs = pack
    base = 40
    parts = ((base - n, up, wup, cup, in_up, (), ws, cs), (base, own, wind, coef, 1.0, lead, None, 0), (base + n, dn, wdn, cdn, in_dn, (), ws, cs))
    for row, st, wd, cf, inside, ld, w, c in parts:
        copy_in(D, row, cf, (c,), 0, n, inside * (C * C))
        copy_in(A, row, cf, (c + 1,), 0, n, inside)
        copy_in(E, row, st, ld + (0,), 0, n, C)
        copy_in(U, row, st, ld + (1,), 0, n)
        copy_in(V, row, st, ld + (2,), 0, n)
        for f, dst in enumerate((W0, W1)):
            copy_in(dst, row, wd, (k, f) if w is None else (w + f,), 0, n, H)

    def prepare(s):
        W0[s] = W0[s] * A[s]
        W1[s] = W1[s] * A[s]
        FY[s] = D[s] * V[s]

    each((E,), base - n, 3 * n, prepare)
    sweep(E, U, V, FY, D, A, (W0, W1), base, n, (in_up, in_dn), 0)
    for f, src in enumerate((E, U, V)):
        for g in range(0, n, 8):
            for c in range(E.shape[0]):
                to = (f, at(g), pl.ds(c * LANES, LANES))
                val = read_own(src, base, g, c)
                if f == 0:
                    val = val * (1.0 / C)
                first[to] = val
                delta[to] = val - guess[(k,) + to]


def relax_b_kernel(n, space_ref, d, up, dn, coef, cup, cdn, res, E, U, V, FY, D, A):
    in_up, in_dn, _, _ = rim_flags(space_ref[0])
    base = 40
    for row, st, cf, inside, c in ((base - n, up, cup, in_up, 5), (base, d, coef, 1.0, 0), (base + n, dn, cdn, in_dn, 5)):
        copy_in(D, row, cf, (c,), 0, n, inside * (C * C))
        copy_in(A, row, cf, (c + 1,), 0, n, inside)
        copy_in(E, row, st, (0,), 0, n, C)
        copy_in(U, row, st, (1,), 0, n)
        copy_in(V, row, st, (2,), 0, n)
    flux_rows(FY, V, D, base - n, 3 * n)
    sweep(E, U, V, FY, D, A, None, base, n, (in_up, in_dn), 0)
    for f, src in enumerate((E, U, V)):
        for g in range(0, n, 8):
            for c in range(E.shape[0]):
                res[f, at(g), pl.ds(c * LANES, LANES)] = read_own(src, base, g, c)


def relax_a_kernel(n, space_ref, d, up, dn, uup, ddn, coef, cup, cdn, cuu, cdd, more, res, total, E, U, V, FY, D, A):
    in_up, in_dn, in_uu, in_dd = rim_flags(space_ref[0])
    base = 48
    for row, rows, st, cf, inside, c in (
        (base - n - 2, 2, uup, cuu, in_uu, 0),
        (base - n, n, up, cup, in_up, 5),
        (base, n, d, coef, 1.0, 0),
        (base + n, n, dn, cdn, in_dn, 5),
        (base + 2 * n, 2, ddn, cdd, in_dd, 0),
    ):
        copy_in(D, row, cf, (c,), 0, rows, inside * (C * C))
        copy_in(A, row, cf, (c + 1,), 0, rows, inside)
        copy_in(E, row, st, (0,), 0, rows, C)
        copy_in(U, row, st, (1,), 0, rows)
        copy_in(V, row, st, (2,), 0, rows)
    flux_rows(FY, V, D, base - n - 8, 3 * n + 16)
    sweep(E, U, V, FY, D, A, None, base, n, (in_up, in_dn), 1)
    for f, src in enumerate((E, U, V)):
        for g in range(0, n, 8):
            for c in range(E.shape[0]):
                res[f, at(g), pl.ds(c * LANES, LANES)] = read_own(src, base, g, c)
    coarse_coefs(D, A, base - 8, n + 16)
    flux_rows(FY, V, D, base - 8, n + 16)
    coarse_step(E, U, V, FY, D, A, base, n, base, n, (in_up, in_dn))
    for f, src in enumerate((E, U, V)):
        for g in range(0, n, 8):
            for c in range(E.shape[0]):
                to = (f, at(g), pl.ds(c * LANES, LANES))
                total[to] = read_own(src, base, g, c) + more[to]


def chain_kernel(n, pos_ref, ca, cb0, cb1, cc, yup, ydn, zup, zdn, coef, cup, cdn, r1, fa, fb, out, E, U, V, FY, D, A, X, Y, Z):
    tm, space = pos_ref[0], pos_ref[1]
    base, halo, half = 24, 16, cb0.shape[1]
    in_up, in_dn, _, _ = rim_flags(space)
    keep = (in_up, in_dn)
    for row, cf, c, start, rows, inside in (
        (base - halo, cup, 5, n - halo, halo, in_up),
        (base, coef, 0, 0, n, 1.0),
        (base + n, cdn, 5, 0, halo, in_dn),
    ):
        copy_in(D, row, cf, (c,), start, rows, inside * (C * C))
        copy_in(A, row, cf, (c + 1,), start, rows, inside)
    coarse_coefs(D, A, base - halo, n + 2 * halo)

    def add(lo, rows):
        def put(s):
            E[s] = E[s] + X[s]
            U[s] = U[s] + Y[s]
            V[s] = V[s] + Z[s]
            FY[s] = D[s] * V[s]

        each((E,), lo, rows, put)

    def coarse(reach):
        coarse_step(E, U, V, FY, D, A, base - reach, n + 2 * reach, base, n, keep)

    use = jnp.where(tm >= 3, 1.0, 0.0)
    for f, dst in enumerate((E, U, V)):
        copy_in(dst, base - 10, yup, (f,), 2, 10, use)
        copy_in(dst, base, cc, (f,), 0, n, use)
        copy_in(dst, base + n, ydn, (f,), 2, 10, use)
    flux_rows(FY, V, D, base - halo, n + 2 * halo)
    coarse(8)
    coarse(6)
    use = jnp.where(tm >= 2, 1.0, 0.0)
    for f, dst in enumerate((X, Y, Z)):
        copy_in(dst, base - 6, zup, (f,), 0, 6, use)
        copy_in(dst, base, cb0, (f,), 0, half, use)
        copy_in(dst, base + half, cb1, (f,), 0, n - half, use)
        copy_in(dst, base + n, zdn, (f,), 0, 6, use)
    add(base - 8, n + 16)
    coarse(4)
    coarse(2)
    use = jnp.where(tm >= 1, 1.0, 0.0)
    for f, dst in enumerate((X, Y, Z)):
        copy_in(dst, base - 2, yup, (f,), 0, 2, use)
        copy_in(dst, base, ca, (f,), 0, n, use)
        copy_in(dst, base + n, ydn, (f,), 0, 2, use)
    add(base - 8, n + 16)

    def write(k, first, more):
        for f, src in enumerate((E, U, V)):
            for g in range(0, n, 8):
                for c in range(E.shape[0]):
                    to = (f, at(g), pl.ds(c * LANES, LANES))
                    val = read_own(src, base, g, c)
                    if more is not None:
                        val = val + more[to]
                    if f == 0:
                        val = val * (1.0 / C)
                    out[(k,) + to] = first[to] + val

    write(0, fa, None)
    coarse(0)
    write(1, fb, r1)


def call(kernel, n, ncols, rows, fields, cost, outs, *args):
    scratch = [pltpu.VMEM((ncols // LANES, rows, LANES), jnp.float32)] * fields
    vmem = pl.BlockSpec(memory_space=pltpu.VMEM)
    return pl.pallas_call(
        lambda *refs: kernel(n, *refs),
        out_shape=outs,
        in_specs=[pl.BlockSpec(memory_space=pltpu.SMEM)] + [vmem] * (len(args) - 1),
        out_specs=jax.tree.map(lambda _: vmem, outs),
        scratch_shapes=scratch,
        compiler_params=pltpu.CompilerParams(vmem_limit_bytes=(ncols * rows * fields) * 4 + 2**21),
        cost_estimate=pl.CostEstimate(flops=cost * 10**6, bytes_accessed=0, transcendentals=0),
    )(*args)


def shards(initial, guess, depth, friction, mask, wind):
    n, ncols = depth.shape
    spaces, times = lax.axis_size("space"), lax.axis_size("tm")
    tm, space = lax.axis_index("tm"), lax.axis_index("space")
    pos = jnp.stack([tm, space]).astype(jnp.int32)
    where = space.astype(jnp.int32)[None]

    def sides(x, hop=1):
        return lax.ppermute(x, "space", ring(spaces, hop)), lax.ppermute(x, "space", ring(spaces, -hop))

    def ends(x, rows, hop=1):
        up = lax.ppermute(x[..., n - rows :, :], "space", ring(spaces, hop))
        dn = lax.ppermute(x[..., :rows, :], "space", ring(spaces, -hop))
        return up, dn

    state = jax.ShapeDtypeStruct((3, n, ncols), jnp.float32)
    coef = jnp.stack([depth, mask.astype(jnp.float32) / (1.0 + H * friction)])

    pack = jnp.concatenate([guess[0], wind[1], coef])
    bu, bd = sides(pack)
    last, _ = lax.optimization_barrier((guess[1], pack))
    earlier = lax.ppermute(last, "tm", ring(times, 1))
    wu, wd = sides(wind[0])
    cuu, cdd = ends(coef, 2, 2)
    entry = jnp.where(tm == 0, initial, earlier)
    au, ad = sides(entry)
    bu, bd, cuu, cdd = lax.optimization_barrier((bu, bd, cuu, cdd))

    fine_b = functools.partial(fine_kernel, 1, ((0,), 3, 5))
    fb, db = call(fine_b, n, ncols, 120, 8, 60, (state, state), where, guess, bu, bd, wind, bu, bd, coef, bu, bd, guess)
    dbu, dbd = sides(db)
    fine_a = functools.partial(fine_kernel, 0, ((), 0, 5))
    fa, da = call(fine_a, n, ncols, 120, 8, 60, (state, state), where, entry, au, ad, wind, wu, wd, coef, bu, bd, guess)
    dau, dad = sides(da)
    dauu, dadd = ends(da, 2, 2)
    rb = call(relax_b_kernel, n, ncols, 120, 6, 60, state, where, db, dbu, dbd, coef, bu, bd)
    ra, c1 = call(relax_a_kernel, n, ncols, 144, 6, 60, (state, state), where, da, dau, dad, dauu, dadd, coef, bu, bd, cuu, cdd, rb)

    ca = lax.ppermute(c1, "tm", ring(times, 1))
    cc = lax.ppermute(c1, "tm", ring(times, -1))
    half = n // 2
    cb0 = lax.ppermute(ca[:, :half], "tm", ring(times, 1))
    cb1 = lax.ppermute(cc[:, half:], "tm", ring(times, -1))

    def skew(x, hop):
        pairs = [(t * spaces + p, (t + 1) % times * spaces + (p + hop) % spaces) for t in range(times) for p in range(spaces)]
        return lax.ppermute(x, ("tm", "space"), pairs)

    zup, zdn = skew(ca[:, -6:], 1), skew(ca[:, :6], -1)
    yup = lax.ppermute(jnp.concatenate([ca[:, -2:], cc[:, -10:]], axis=1), "space", ring(spaces, 1))
    ydn = lax.ppermute(jnp.concatenate([ca[:, :2], cc[:, :10]], axis=1), "space", ring(spaces, -1))
    out = jax.ShapeDtypeStruct(guess.shape, jnp.float32)
    return call(
        chain_kernel, n, ncols, 88, 9, 20, out, pos, ca, cb0, cb1, cc, yup, ydn, zup, zdn, coef, bu, bd, ra, fa, fb
    )


def solution(mesh):
    return jax.shard_map(
        shards,
        mesh=mesh,
        in_specs=(
            P(None, "space", None),
            P("tm", None, "space", None),
            P("space", None),
            P("space", None),
            P("space", None),
            P("tm", None, "space", None),
        ),
        out_specs=P("tm", None, "space", None),
        check_vma=False,
    )
```

```python
import functools

import jax
import jax.numpy as jnp
from jax import lax
from jax.experimental import pallas as pl
from jax.experimental.pallas import tpu as pltpu
from jax.sharding import PartitionSpec as P

FACTOR = 16
H = 0.05
C = 0.5 * H
LANES = 128
SWEEP = 8000


def ring(n, shift):
    return [(i, (i + shift) % n) for i in range(n)]


def at(r, rows=8):
    return pl.ds(r, rows)


FOLD = 4


def diff_cols(chunks):
    lane = lax.broadcasted_iota(jnp.int32, (8, LANES), 1)
    first, last = lane == 0, lane == LANES - 1
    blocks = len(chunks) // FOLD
    left = [pltpu.roll(chunks[b * FOLD + FOLD - 1], 1, 1) for b in range(blocks)]
    right = [pltpu.roll(chunks[b * FOLD], LANES - 1, 1) for b in range(blocks)]
    out = []
    for b in range(blocks):
        for j in range(FOLD):
            c = b * FOLD + j
            lo = chunks[c - 1] if j > 0 else jnp.where(first, left[b - 1] if b > 0 else 0.0, left[b])
            hi = chunks[c + 1] if j < FOLD - 1 else jnp.where(last, right[b + 1] if b + 1 < blocks else 0.0, right[b])
            out.append(hi - lo)
    return out


def fold(chunks):
    lane = lax.broadcasted_iota(jnp.int32, (8, LANES), 1)
    width = LANES // FOLD
    out = []
    for b in range(0, len(chunks), FOLD):
        for j in range(FOLD):
            index = lane * FOLD % LANES + j
            val = jnp.take_along_axis(chunks[b], index, axis=1)
            for k in range(1, FOLD):
                val = jnp.where(lane >= k * width, jnp.take_along_axis(chunks[b + k], index, axis=1), val)
            out.append(val)
    return out


def unfold(chunks):
    lane = lax.broadcasted_iota(jnp.int32, (8, LANES), 1)
    width = LANES // FOLD
    out = []
    for b in range(0, len(chunks), FOLD):
        for k in range(FOLD):
            index = lane // FOLD + k * width
            val = jnp.take_along_axis(chunks[b], index, axis=1)
            for j in range(1, FOLD):
                val = jnp.where(lane % FOLD == j, jnp.take_along_axis(chunks[b + j], index, axis=1), val)
            out.append(val)
    return out


def copy_in(dst, base, src, index, rows, scale=None):
    for g in range(rows // 8):
        for c in range(dst.shape[0]):
            val = src[index(g) + (pl.ds(c * LANES, LANES),)]
            dst[c, at(pl.multiple_of(base + g * 8, 8)), :] = val if scale is None else val * scale


def plane(f, start=0):
    return lambda g: (f, at(start + g * 8))


def copy_rows(dst, base, src, f, start, rows, scale):
    for g in range(0, rows, 8):
        count = min(8, rows - g)
        for c in range(dst.shape[0]):
            dst[c, at(base + g, count), :] = src[f, at(start + g, count), pl.ds(c * LANES, LANES)] * scale


def each(fields, base, rows, f):
    def group(g, _):
        for c in range(fields[0].shape[0]):
            f((c, at(base + g * 8), slice(None)))
        return 0

    lax.fori_loop(0, rows // 8, group, 0)


def flux_rows(FY, V, D, base, rows):
    def put(s):
        FY[s] = D[s] * V[s]

    each((FY,), base, rows, put)


def level_pass(E, U, FY, D, r):
    cs = range(E.shape[0])
    dx = diff_cols([D[c, at(r), :] * U[c, at(r), :] for c in cs])
    for c in cs:
        E[c, at(r), :] = E[c, at(r), :] - (dx[c] + (FY[c, at(r + 1), :] - FY[c, at(r - 1), :]))


def velocity_pass(E, U, V, FY, D, A, W, r, gain=None):
    cs = range(E.shape[0])
    dx = diff_cols([E[c, at(r), :] for c in cs])
    for c in cs:
        s = (c, at(r), slice(None))
        dy = E[c, at(r + 1), :] - E[c, at(r - 1), :]
        gx = dx[c]
        if gain is not None:
            gx, dy = gx * gain, dy * gain
        u = A[s] * (U[s] - gx)
        v = A[s] * (V[s] - dy)
        if W is not None:
            u, v = u + W[0][s], v + W[1][s]
        U[s] = u
        V[s] = v
        FY[s] = D[s] * v


def keep_rim(E, base, n, keep):
    for r, k in ((base - 1, keep[0]), (base + n, keep[1])):
        for c in range(E.shape[0]):
            E[c, at(r, 1), :] = E[c, at(r, 1), :] * k


def sweep(E, U, V, FY, D, A, W, base, n, keep, wide):
    for phase in range(FACTOR // 4):
        reach = 2 * FACTOR - 8 * phase
        lo, groups = base - reach, (n + 2 * reach) // 8

        def step(_, carry, lo=lo, groups=groups):
            for g in range(groups + wide):
                level_pass(E, U, FY, D, lo - wide + g * 8)
            keep_rim(E, base, n, keep)
            for g in range(groups):
                velocity_pass(E, U, V, FY, D, A, W, lo + g * 8)
            return carry

        lax.fori_loop(0, 4, step, 0)


def coarse_coefs(D, A, base, rows):
    def put(s):
        D[s] = D[s] * float(FACTOR)
        A[s] = A[s] / (float(FACTOR) - (FACTOR - 1.0) * A[s])

    each((D, A), base, rows, put)


def coarse_step(E, U, V, FY, D, A, lo, rows, base, n, keep):
    for r in range(lo - 1, lo + rows + 1, 8):
        level_pass(E, U, FY, D, r)
    keep_rim(E, base, n, keep)
    for r in range(lo, lo + rows, 8):
        velocity_pass(E, U, V, FY, D, A, None, r, float(FACTOR))


def place(space):
    size = lax.axis_size("space")
    even = lax.rem(space, 2) == 0
    keep = tuple(jnp.where(x, 1.0, 0.0) for x in (space > 0, space < size - 1))
    return even, keep, keep[0] * keep[1]


def read_own(src, base, g, c):
    return src[c, at(base + g), :]


def sides_of(even, base, n):
    return jnp.where(even, base - n, base + n), jnp.where(even, base + n, base - n)


def folded(raw, k, out, f, n):
    def group(g, _):
        rows = at(pl.multiple_of(g * 8, 8))
        cs = range(raw.shape[2] // LANES)
        for c, val in enumerate(fold([raw[k, rows, pl.ds(c * LANES, LANES)] for c in cs])):
            out[f, rows, pl.ds(c * LANES, LANES)] = val
        return 0

    lax.fori_loop(0, n // 8, group, 0)


def main_kernel(n, guess, wind, depth, friction, mask, out, raw, land, sems):
    copies = [
        pltpu.make_async_copy(src, dst, sems.at[i])
        for i, (src, dst) in enumerate(
            (
                (guess.at[0], raw.at[pl.ds(0, 3)]),
                (wind.at[1], raw.at[pl.ds(3, 2)]),
                (depth, raw.at[5]),
                (friction, raw.at[6]),
                (mask, land),
            )
        )
    ]
    for copy in copies:
        copy.start()
    for copy in copies:
        copy.wait()
    raw[6] = land[...].astype(jnp.float32) / (1.0 + H * raw[6])
    for f in range(7):
        folded(raw, f, out, f, n)


def late_kernel(n, guess, wind, initial, _, last, late, raw, sems):
    copies = [
        pltpu.make_async_copy(src, dst, sems.at[i])
        for i, (src, dst) in enumerate(
            ((guess.at[1], raw.at[pl.ds(0, 3)]), (initial, raw.at[pl.ds(3, 3)]), (wind.at[0], raw.at[pl.ds(6, 2)]))
        )
    ]
    for copy in copies:
        copy.start()
    for copy in copies:
        copy.wait()
    for f in range(8):
        folded(raw, f, last if f < 3 else late, f if f < 3 else f - 3, n)


def fine_kernel(n, space_ref, own, across, beside, coef, coef_a, coef_b, nxt, *refs):
    outs, (E, U, V, FY, D, A, W0, W1) = refs[:-8], refs[-8:]
    first, delta = outs[:2]
    even, keep, inside = place(space_ref[0])
    base = 40
    row_a, row_b = sides_of(even, base, n)
    for row, st, cf, ok in ((row_a, across, coef_a, inside), (base, own, coef, 1.0), (row_b, beside, coef_b, 1.0)):
        copy_in(D, row, cf, plane(5), n, ok * (C * C))
        copy_in(A, row, cf, plane(6), n, ok)
        copy_in(E, row, st, plane(0), n, C)
        copy_in(U, row, st, plane(1), n)
        copy_in(V, row, st, plane(2), n)
        copy_in(W0, row, st, plane(3), n, H)
        copy_in(W1, row, st, plane(4), n, H)

    def prepare(s):
        W0[s] = W0[s] * A[s]
        W1[s] = W1[s] * A[s]
        FY[s] = D[s] * V[s]

    each((E,), base - n, 3 * n, prepare)
    sweep(E, U, V, FY, D, A, (W0, W1), base, n, keep, 0)
    for f, src in enumerate((E, U, V)):
        for g in range(0, n, 8):
            for c in range(E.shape[0]):
                to = (f, at(g), pl.ds(c * LANES, LANES))
                val = read_own(src, base, g, c)
                if f == 0:
                    val = val * (1.0 / C)
                first[to] = val
                val = val - nxt[to]
                delta[to] = val
                if len(outs) > 2:
                    outs[2][f * (n // 8) + g // 8, :, pl.ds(c * LANES, LANES)] = val
    if len(outs) > 2:
        for f in range(2):
            outs[2][3 * (n // 8) + f] = jnp.where(even, coef_a[5 + f, at(n - 8), :], coef_a[5 + f, at(0), :])


def relax_b_kernel(n, space_ref, d, across, beside, coef, coef_a, coef_b, res, E, U, V, FY, D, A):
    even, keep, inside = place(space_ref[0])
    base = 40
    row_a, row_b = sides_of(even, base, n)

    def grouped(f):
        return lambda g: (f * (n // 8) + g, slice(None))

    for row, st, cf, ok, index in (
        (row_a, across, coef_a, inside, plane),
        (base, d, coef, 1.0, plane),
        (row_b, beside, coef_b, 1.0, grouped),
    ):
        copy_in(D, row, cf, plane(5), n, ok * (C * C))
        copy_in(A, row, cf, plane(6), n, ok)
        copy_in(E, row, st, index(0), n, C)
        copy_in(U, row, st, index(1), n)
        copy_in(V, row, st, index(2), n)
    flux_rows(FY, V, D, base - n, 3 * n)
    sweep(E, U, V, FY, D, A, None, base, n, keep, 0)
    for f, src in enumerate((E, U, V)):
        for g in range(0, n, 8):
            for c in range(E.shape[0]):
                res[f, at(g), pl.ds(c * LANES, LANES)] = read_own(src, base, g, c)


def relay_kernel(n, space_ref, d, across, out):
    even, _, _ = place(space_ref[0])
    groups = n // 8
    for f in range(3):
        for g in range(groups):
            out[f * groups + g] = d[f, at(g * 8), :]
        out[3 * groups + f] = jnp.where(even, across[f, at(n - 8), :], across[f, at(0), :])


def relax_a_kernel(n, space_ref, d, across, beside, coef, coef_a, coef_b, relay, more, res, total, E, U, V, FY, D, A):
    space = space_ref[0]
    even, keep, inside = place(space)
    base = 48
    row_a, row_b = sides_of(even, base, n)
    row_c = jnp.where(even, base + 2 * n, base - n - 8)
    inside_c = jnp.where(even, jnp.where(space < lax.axis_size("space") - 2, 1.0, 0.0), jnp.where(space > 1, 1.0, 0.0))
    groups = n // 8

    def grouped(f):
        return lambda g: (f * groups + g, slice(None))

    for row, st, cf, ok, index in (
        (row_a, across, coef_a, inside, plane),
        (base, d, coef, 1.0, plane),
        (row_b, beside, coef_b, 1.0, grouped),
    ):
        copy_in(D, row, cf, plane(5), n, ok * (C * C))
        copy_in(A, row, cf, plane(6), n, ok)
        copy_in(E, row, st, index(0), n, C)
        copy_in(U, row, st, index(1), n)
        copy_in(V, row, st, index(2), n)

    def one(k):
        return lambda g: (k, slice(None))

    copy_in(D, row_c, relay, one(3 * groups), 8, inside_c * (C * C))
    copy_in(A, row_c, relay, one(3 * groups + 1), 8, inside_c)
    copy_in(E, row_c, beside, one(3 * groups), 8, C)
    copy_in(U, row_c, beside, one(3 * groups + 1), 8)
    copy_in(V, row_c, beside, one(3 * groups + 2), 8)
    flux_rows(FY, V, D, base - n - 8, 3 * n + 16)
    sweep(E, U, V, FY, D, A, None, base, n, keep, 1)
    for f, src in enumerate((E, U, V)):
        for g in range(0, n, 8):
            for c in range(E.shape[0]):
                res[f, at(g), pl.ds(c * LANES, LANES)] = read_own(src, base, g, c)
    coarse_coefs(D, A, base - 8, n + 16)
    flux_rows(FY, V, D, base - 8, n + 16)
    coarse_step(E, U, V, FY, D, A, base, n, base, n, keep)
    for f, src in enumerate((E, U, V)):
        for g in range(0, n, 8):
            for c in range(E.shape[0]):
                to = (f, at(g), pl.ds(c * LANES, LANES))
                total[to] = read_own(src, base, g, c) + more[to]


RIMS = (2, 6, 10)


def chain_kernel(n, pos_ref, ca, cc, p1, p2, p3, coef, coef_a, coef_b, r1, fa, fb, out, E, U, V, FY, D, A, X, Y, Z):
    tm, space = pos_ref[0], pos_ref[1]
    base, halo = 24, 16
    main, rest = p1.shape[1] - 2 * RIMS[0], p2.shape[1] - 2 * RIMS[2]
    even, keep, inside = place(space)
    odd = jnp.logical_not(even)
    for cond, up, dn, ok_up, ok_dn in ((even, coef_a, coef_b, inside, 1.0), (odd, coef_b, coef_a, 1.0, inside)):

        @pl.when(cond)
        def _(up=up, dn=dn, ok_up=ok_up, ok_dn=ok_dn):
            for f, dst, k in ((5, D, C * C), (6, A, 1.0)):
                copy_in(dst, base - halo, up, plane(f, n - halo), halo, ok_up * k)
                copy_in(dst, base + n, dn, plane(f), halo, ok_dn * k)

    copy_in(D, base, coef, plane(5), n, C * C)
    copy_in(A, base, coef, plane(6), n)
    coarse_coefs(D, A, base - halo, n + 2 * halo)

    def rims(fields, k, src, start, use):
        rows = RIMS[k]
        for f, dst in enumerate(fields):
            copy_rows(dst, base - rows, src, f, start, rows, use)
            copy_rows(dst, base + n, src, f, start + rows, rows, use)

    def add(lo, rows):
        def put(s):
            E[s] = E[s] + X[s]
            U[s] = U[s] + Y[s]
            V[s] = V[s] + Z[s]
            FY[s] = D[s] * V[s]

        each((E,), lo, rows, put)

    def coarse(reach):
        coarse_step(E, U, V, FY, D, A, base - reach, n + 2 * reach, base, n, keep)

    use = jnp.where(tm >= 3, 1.0, 0.0)
    rims((E, U, V), 2, p2, rest, use)
    for f, dst in enumerate((E, U, V)):
        copy_in(dst, base, cc, plane(f), n, use)
    flux_rows(FY, V, D, base - halo, n + 2 * halo)
    coarse(8)
    coarse(6)
    use = jnp.where(tm >= 2, 1.0, 0.0)
    rims((X, Y, Z), 1, p3, 0, use)
    for f, dst in enumerate((X, Y, Z)):
        copy_in(dst, base, p1, plane(f), main, use)
        copy_in(dst, base + main, p2, plane(f), rest, use)
    add(base - 8, n + 16)
    coarse(4)
    coarse(2)
    use = jnp.where(tm >= 1, 1.0, 0.0)
    rims((X, Y, Z), 0, p1, main, use)
    for f, dst in enumerate((X, Y, Z)):
        copy_in(dst, base, ca, plane(f), n, use)
    add(base - 8, n + 16)

    def write(k, first, more):
        for f, src in enumerate((E, U, V)):

            def group(g, carry, f=f, src=src):
                rows = pl.multiple_of(g * 8, 8)
                vals = []
                for c in range(E.shape[0]):
                    to = (f, at(rows), pl.ds(c * LANES, LANES))
                    val = read_own(src, base, rows, c)
                    if more is not None:
                        val = val + more[to]
                    if f == 0:
                        val = val * (1.0 / C)
                    vals.append(first[to] + val)
                for c, val in enumerate(unfold(vals)):
                    out[k, f, at(rows), pl.ds(c * LANES, LANES)] = val
                return carry

            lax.fori_loop(0, n // 8, group, 0)

    write(0, fa, None)
    coarse(0)
    write(1, fb, r1)


def call(kernel, n, ncols, rows, fields, cost, outs, *args, after=()):
    scratch = [pltpu.VMEM((ncols // LANES, rows, LANES), jnp.float32)] * fields
    vmem = pl.BlockSpec(memory_space=pltpu.VMEM)
    return pl.pallas_call(
        lambda *refs: kernel(n, *refs[: len(args)], *refs[len(args) + len(after) :]),
        out_shape=outs,
        in_specs=[pl.BlockSpec(memory_space=pltpu.SMEM)] + [vmem] * (len(args) - 1) + [pl.BlockSpec(memory_space=pl.ANY)] * len(after),
        out_specs=jax.tree.map(lambda _: vmem, outs),
        scratch_shapes=scratch,
        compiler_params=pltpu.CompilerParams(vmem_limit_bytes=(ncols * rows * fields) * 4 + 2**21),
        cost_estimate=pl.CostEstimate(flops=cost * 10**6, bytes_accessed=0, transcendentals=0),
    )(*args, *after)


def packed(kernel, n, ncols, fields, scratch, *args):
    def block(k):
        return jax.ShapeDtypeStruct((k, n, ncols), jnp.float32)

    return pl.pallas_call(
        functools.partial(kernel, n),
        out_shape=[block(k) for k in fields],
        in_specs=[pl.BlockSpec(memory_space=pl.ANY)] * len(args),
        out_specs=[pl.BlockSpec(memory_space=pltpu.VMEM)] * len(fields),
        scratch_shapes=[pltpu.VMEM(x.shape, x.dtype) for x in scratch] + [pltpu.SemaphoreType.DMA((len(args),))],
        compiler_params=pltpu.CompilerParams(vmem_limit_bytes=4 * 2**20),
    )(*args)


def shards(initial, guess, depth, friction, mask, wind):
    n, ncols = depth.shape
    spaces, times = lax.axis_size("space"), lax.axis_size("tm")
    tm, space = lax.axis_index("tm"), lax.axis_index("space")
    pos = jnp.stack([tm, space]).astype(jnp.int32)
    where = space.astype(jnp.int32)[None]
    even = space % 2 == 0

    def across(x):
        return lax.ppermute(x, "space", [(i, (i - 1 if i % 2 == 0 else i + 1) % spaces) for i in range(spaces)])

    def beside(x):
        return lax.ppermute(x, "space", [(i, i ^ 1) for i in range(spaces)])

    state = jax.ShapeDtypeStruct((3, n, ncols), jnp.float32)
    both = jax.ShapeDtypeStruct((3 * (n // 8) + 2, 8, ncols), jnp.float32)
    raw = jax.ShapeDtypeStruct((8, n, ncols), jnp.float32)
    (b_own,) = packed(main_kernel, n, ncols, (7,), (raw, mask), guess, wind, depth, friction, mask)
    b_a, b_b = across(b_own), beside(b_own)
    last, late = packed(late_kernel, n, ncols, (3, 5), (raw,), guess, wind, initial, b_own)
    earlier = lax.ppermute(last, "tm", ring(times, 1))
    a_own = jnp.concatenate([jnp.where(tm == 0, late[:3], earlier), late[3:]])
    a_a, a_b = across(a_own), beside(a_own)

    fb, db, db_pack = call(fine_kernel, n, ncols, 120, 8, SWEEP, (state, state, both), where, b_own, b_a, b_b, b_own, b_a, b_b, last)
    db_a, db_b = across(db), beside(db_pack)
    fa, da = call(fine_kernel, n, ncols, 120, 8, SWEEP, (state, state), where, a_own, a_a, a_b, b_own, b_a, b_b, b_own, after=(db,))
    da_a = across(da)
    rb = call(relax_b_kernel, n, ncols, 120, 6, SWEEP, state, where, db, db_a, db_b, b_own, b_a, b_b, after=(da,))
    more = jax.ShapeDtypeStruct((3 * (n // 8) + 3, 8, ncols), jnp.float32)
    da_b = beside(call(relay_kernel, n, ncols, 8, 0, 1, more, where, da, da_a, after=(rb,)))
    ra, c1 = call(relax_a_kernel, n, ncols, 144, 6, SWEEP, (state, state), where, da, da_a, da_b, b_own, b_a, b_b, db_b, rb)

    ca = lax.ppermute(c1, "tm", ring(times, 1))
    cc = lax.ppermute(c1, "tm", ring(times, -1))
    rim_a = across(jnp.where(even, c1[:, : RIMS[2]], c1[:, -RIMS[2] :]))
    rim_b = beside(jnp.where(even, c1[:, -RIMS[2] :], c1[:, : RIMS[2]]))
    up, dn = jnp.where(even, rim_a, rim_b), jnp.where(even, rim_b, rim_a)
    main = n - 8
    p1 = jnp.concatenate([ca[:, :main], up[:, -RIMS[0] :], dn[:, : RIMS[0]]], axis=1)
    p2 = jnp.concatenate([cc[:, main:], up, dn], axis=1)
    p3 = jnp.concatenate([up[:, -RIMS[1] :], dn[:, : RIMS[1]]], axis=1)
    p1 = lax.ppermute(p1, "tm", ring(times, 1))
    p2 = lax.ppermute(p2, "tm", ring(times, -1))
    p3 = lax.ppermute(p3, "tm", ring(times, 2))
    out = jax.ShapeDtypeStruct(guess.shape, jnp.float32)
    return call(
        chain_kernel, n, ncols, 88, 9, SWEEP // 2, out, pos, ca, cc, p1, p2, p3, b_own, b_a, b_b, ra, fa, fb
    )


def solution(mesh):
    return jax.shard_map(
        shards,
        mesh=mesh,
        in_specs=(
            P(None, "space", None),
            P("tm", None, "space", None),
            P("space", None),
            P("space", None),
            P("space", None),
            P("tm", None, "space", None),
        ),
        out_specs=P("tm", None, "space", None),
        check_vma=False,
    )
```

```python
import functools

import jax
import jax.numpy as jnp
from jax import lax
from jax.experimental import pallas as pl
from jax.experimental.pallas import tpu as pltpu
from jax.sharding import PartitionSpec as P

FACTOR = 16
H = 0.05
C = 0.5 * H
LANES = 128
SWEEP = 8000


def ring(n, shift):
    return [(i, (i + shift) % n) for i in range(n)]


def at(r, rows=8):
    return pl.ds(r, rows)


FOLD = 4


def diff_cols(chunks):
    lane = lax.broadcasted_iota(jnp.int32, (8, LANES), 1)
    first, last = lane == 0, lane == LANES - 1
    blocks = len(chunks) // FOLD
    left = [pltpu.roll(chunks[b * FOLD + FOLD - 1], 1, 1) for b in range(blocks)]
    right = [pltpu.roll(chunks[b * FOLD], LANES - 1, 1) for b in range(blocks)]
    out = []
    for b in range(blocks):
        for j in range(FOLD):
            c = b * FOLD + j
            lo = chunks[c - 1] if j > 0 else jnp.where(first, left[b - 1] if b > 0 else 0.0, left[b])
            hi = chunks[c + 1] if j < FOLD - 1 else jnp.where(last, right[b + 1] if b + 1 < blocks else 0.0, right[b])
            out.append(hi - lo)
    return out


def order_matrix(inverse):
    size = FOLD * LANES
    place = lax.broadcasted_iota(jnp.int32, (size, size), 0 if inverse else 1)
    column = lax.broadcasted_iota(jnp.int32, (size, size), 1 if inverse else 0)
    return jnp.where(place % LANES * FOLD + place // LANES == column, 1.0, 0.0).astype(jnp.bfloat16)


def reorder(src, dst, matrix, index):
    size = matrix.shape[0]
    for b in range(0, src.shape[-1], size):
        val = src[index + (slice(None), pl.ds(b, size))]
        shape = val.shape
        val = val.reshape(-1, size)
        total = None
        for _ in range(3):
            part = val.astype(jnp.bfloat16)
            val = val - part.astype(jnp.float32)
            piece = jnp.dot(part, matrix[...], preferred_element_type=jnp.float32)
            total = piece if total is None else total + piece
        dst[index + (slice(None), pl.ds(b, size))] = total.reshape(shape)


def copy_in(dst, base, src, index, rows, scale=None):
    for g in range(rows // 8):
        for c in range(dst.shape[0]):
            val = src[index(g) + (pl.ds(c * LANES, LANES),)]
            dst[c, at(pl.multiple_of(base + g * 8, 8)), :] = val if scale is None else val * scale


def plane(f, start=0):
    return lambda g: (f, at(start + g * 8))


def copy_rows(dst, base, src, f, start, rows, scale=1.0):
    for g in range(0, rows, 8):
        count = min(8, rows - g)
        for c in range(dst.shape[0]):
            dst[c, at(base + g, count), :] = src[f, at(start + g, count), pl.ds(c * LANES, LANES)] * scale


def each(fields, base, rows, f):
    def group(g, _):
        for c in range(fields[0].shape[0]):
            f((c, at(base + g * 8), slice(None)))
        return 0

    lax.fori_loop(0, rows // 8, group, 0)


def flux_rows(FY, V, D, base, rows):
    def put(s):
        FY[s] = D[s] * V[s]

    each((FY,), base, rows, put)


def level_pass(E, U, FY, D, r):
    cs = range(E.shape[0])
    dx = diff_cols([D[c, at(r), :] * U[c, at(r), :] for c in cs])
    for c in cs:
        E[c, at(r), :] = E[c, at(r), :] - (dx[c] + (FY[c, at(r + 1), :] - FY[c, at(r - 1), :]))


def velocity_pass(E, U, V, FY, D, A, W, r, gain=None):
    cs = range(E.shape[0])
    dx = diff_cols([E[c, at(r), :] for c in cs])
    for c in cs:
        s = (c, at(r), slice(None))
        dy = E[c, at(r + 1), :] - E[c, at(r - 1), :]
        gx = dx[c]
        if gain is not None:
            gx, dy = gx * gain, dy * gain
        u = A[s] * (U[s] - gx)
        v = A[s] * (V[s] - dy)
        if W is not None:
            u, v = u + W[0][s], v + W[1][s]
        U[s] = u
        V[s] = v
        FY[s] = D[s] * v


def keep_rim(E, base, n, keep):
    for r, k in ((base - 1, keep[0]), (base + n, keep[1])):
        for c in range(E.shape[0]):
            E[c, at(r, 1), :] = E[c, at(r, 1), :] * k


def sweep(E, U, V, FY, D, A, W, base, n, keep):
    for phase in range(FACTOR // 4):
        reach = 2 * FACTOR - 8 * phase
        lo, groups = base - reach, (n + 2 * reach) // 8

        def step(_, carry, lo=lo, groups=groups):
            for g in range(groups):
                level_pass(E, U, FY, D, lo + g * 8)
            keep_rim(E, base, n, keep)
            for g in range(groups):
                velocity_pass(E, U, V, FY, D, A, W, lo + g * 8)
            return carry

        lax.fori_loop(0, 4, step, 0)


def coarse_coefs(D, A, base, rows):
    def put(s):
        D[s] = D[s] * float(FACTOR)
        A[s] = A[s] / (float(FACTOR) - (FACTOR - 1.0) * A[s])

    each((D, A), base, rows, put)


def coarse_step(E, U, V, FY, D, A, lo, rows, base, n, keep):
    for r in range(lo - 1, lo + rows + 1, 8):
        level_pass(E, U, FY, D, r)
    keep_rim(E, base, n, keep)
    for r in range(lo, lo + rows, 8):
        velocity_pass(E, U, V, FY, D, A, None, r, float(FACTOR))


def inside_grid(space):
    return tuple(jnp.where(x, 1.0, 0.0) for x in (space > 0, space < lax.axis_size("space") - 1))


def read_own(src, base, g, c):
    return src[c, at(base + g), :]


def main_kernel(n, guess, wind, initial, depth, friction, mask, out, last, late, raw, land, matrix, sems):
    copies = [
        pltpu.make_async_copy(src, dst, sems.at[i])
        for i, (src, dst) in enumerate(
            (
                (guess.at[0], raw.at[pl.ds(0, 3)]),
                (wind.at[1], raw.at[pl.ds(3, 2)]),
                (depth, raw.at[5]),
                (friction, raw.at[6]),
                (mask, land),
                (guess.at[1], last),
                (initial, late.at[pl.ds(0, 3)]),
                (wind.at[0], late.at[pl.ds(3, 2)]),
            )
        )
    ]
    for copy in copies:
        copy.start()
    matrix[...] = order_matrix(False)
    for copy in copies:
        copy.wait()
    raw[6] = land[...].astype(jnp.float32) / (1.0 + H * raw[6])
    reorder(raw, out, matrix, (slice(None),))


def late_kernel(n, pos_ref, earlier, last_raw, late_raw, late, last, raw, matrix):
    matrix[...] = order_matrix(False)
    raw[pl.ds(0, 3)] = jnp.where(pos_ref[0] == 0, late_raw[pl.ds(0, 3)], earlier[...])
    raw[pl.ds(3, 2)] = late_raw[pl.ds(3, 2)]
    reorder(raw, late, matrix, (slice(None),))
    reorder(last_raw, last, matrix, (slice(None),))


def load(n, base, keep, state, coefs, fields):
    E, U, V, D, A = fields
    for row, st, cf, ok in zip((base, base - n, base + n), state, coefs, (1.0, *keep)):
        copy_in(D, row, cf, plane(5), n, ok * (C * C))
        copy_in(A, row, cf, plane(6), n, ok)
        copy_in(E, row, st, plane(0), n, C)
        copy_in(U, row, st, plane(1), n)
        copy_in(V, row, st, plane(2), n)


def fine_kernel(n, space_ref, own, up, dn, coef, coef_up, coef_dn, nxt, delta, E, U, V, FY, D, A, W0, W1):
    keep = inside_grid(space_ref[0])
    base = 40
    load(n, base, keep, (own, up, dn), (coef, coef_up, coef_dn), (E, U, V, D, A))
    for row, st in ((base, own), (base - n, up), (base + n, dn)):
        copy_in(W0, row, st, plane(3), n, H)
        copy_in(W1, row, st, plane(4), n, H)

    def prepare(s):
        W0[s] = W0[s] * A[s]
        W1[s] = W1[s] * A[s]
        FY[s] = D[s] * V[s]

    each((E,), base - n, 3 * n, prepare)
    sweep(E, U, V, FY, D, A, (W0, W1), base, n, keep)
    for f, src in enumerate((E, U, V)):
        for g in range(0, n, 8):
            for c in range(E.shape[0]):
                to = (f, at(g), pl.ds(c * LANES, LANES))
                val = read_own(src, base, g, c)
                if f == 0:
                    val = val * (1.0 / C)
                delta[to] = val - nxt[to]


def relax(n, space_ref, state, coefs, fields):
    E, U, V, FY, D, A = fields
    keep = inside_grid(space_ref[0])
    base = 40
    load(n, base, keep, state, coefs, (E, U, V, D, A))
    flux_rows(FY, V, D, base - n, 3 * n)
    sweep(E, U, V, FY, D, A, None, base, n, keep)
    return base


def relax_b_kernel(n, space_ref, d, up, dn, coef, coef_up, coef_dn, res, E, U, V, FY, D, A):
    base = relax(n, space_ref, (d, up, dn), (coef, coef_up, coef_dn), (E, U, V, FY, D, A))
    copy_out(res, (E, U, V), base, n)


def relax_a_kernel(n, space_ref, d, up, dn, coef, coef_up, coef_dn, d_next, nxt, res, fine, next_fine, E, U, V, FY, D, A):
    base = relax(n, space_ref, (d, up, dn), (coef, coef_up, coef_dn), (E, U, V, FY, D, A))
    for f, src in enumerate((E, U, V)):
        for g in range(0, n, 8):
            for c in range(E.shape[0]):
                to = (f, at(g), pl.ds(c * LANES, LANES))
                val = read_own(src, base, g, c)
                res[to] = val
                if f == 0:
                    val = val * (1.0 / C)
                fine[to] = d[to] + coef[to]
                next_fine[to] = d_next[to] + nxt[to] + val


def copy_out(dst, src, base, rows):
    for f, field in enumerate(src):
        for g in range(0, rows, 8):
            count = min(8, rows - g)
            for c in range(field.shape[0]):
                dst[f, at(g, count), pl.ds(c * LANES, LANES)] = field[c, at(base + g, count), :]


HALO = 16
RIMS = (2, 6, 10)


def coarse_load(n, base, keep, coefs, D, A):
    coef, up, dn = coefs
    for row, cf, start, rows, ok in ((base - HALO, up, n - HALO, HALO, keep[0]), (base, coef, 0, n, 1.0), (base + n, dn, 0, HALO, keep[1])):
        copy_in(D, row, cf, plane(5, start), rows, ok * (C * C))
        copy_in(A, row, cf, plane(6, start), rows, ok)
    coarse_coefs(D, A, base - HALO, n + 2 * HALO)


def source_kernel(n, pos_ref, ra, rb, up, dn, coef, coef_up, coef_dn, out, E, U, V, FY, D, A, X, Y, Z):
    base, rim = 24, RIMS[2]
    keep = inside_grid(pos_ref[1])
    coarse_load(n, base, keep, (coef, coef_up, coef_dn), D, A)
    for fields, own, start, rows in (((E, U, V), ra, 0, rim + 2), ((X, Y, Z), rb, rim + 2, rim)):
        for f, dst in enumerate(fields):
            copy_rows(dst, base - rows, up, f, start, rows)
            copy_in(dst, base, own, plane(f), n)
            copy_rows(dst, base + n, dn, f, start, rows)
    flux_rows(FY, V, D, base - HALO, n + 2 * HALO)
    coarse_step(E, U, V, FY, D, A, base - rim, n + 2 * rim, base, n, keep)
    for f, (src, more) in enumerate(((E, X), (U, Y), (V, Z))):
        for g in range(0, n + 2 * rim, 8):
            rows = min(8, n + 2 * rim - g)
            for c in range(E.shape[0]):
                s = (c, at(base - rim + g, rows), slice(None))
                out[f, at(g, rows), pl.ds(c * LANES, LANES)] = src[s] + more[s]


def chain_kernel(n, pos_ref, ca, cc, p1, p2, coef, coef_up, coef_dn, fa, fb, out, E, U, V, FY, D, A, X, Y, Z, result, matrix):
    tm = pos_ref[0]
    base, last, middle = 24, RIMS[2], RIMS[1]
    matrix[...] = order_matrix(True)
    keep = inside_grid(pos_ref[1])
    coarse_load(n, base, keep, (coef, coef_up, coef_dn), D, A)

    def add():
        def put(s):
            E[s] = E[s] + X[s]
            U[s] = U[s] + Y[s]
            V[s] = V[s] + Z[s]
            FY[s] = D[s] * V[s]

        each((E,), base - 8, n + 16, put)

    def coarse(reach):
        coarse_step(E, U, V, FY, D, A, base - reach, n + 2 * reach, base, n, keep)

    use = jnp.where(tm >= 3, 1.0, 0.0)
    for f, dst in enumerate((E, U, V)):
        copy_rows(dst, base - last, cc, f, 0, n + 2 * last, use)
    flux_rows(FY, V, D, base - HALO, n + 2 * HALO)
    coarse(8)
    coarse(6)
    use = jnp.where(tm >= 2, 1.0, 0.0)
    for f, dst in enumerate((X, Y, Z)):
        copy_rows(dst, base - middle, p1, f, 0, p1.shape[1], use)
        copy_rows(dst, base - middle + p1.shape[1], p2, f, 0, p2.shape[1], use)
    add()
    coarse(4)
    coarse(2)
    use = jnp.where(tm >= 1, 1.0, 0.0)
    for f, dst in enumerate((X, Y, Z)):
        copy_rows(dst, base - last, ca, f, 0, n + 2 * last, use)
    add()

    def write(k, first):
        for f, src in enumerate((E, U, V)):
            for g in range(0, n, 8):
                for c in range(E.shape[0]):
                    to = (f, at(g), pl.ds(c * LANES, LANES))
                    val = read_own(src, base, g, c)
                    if f == 0:
                        val = val * (1.0 / C)
                    result[(k,) + to] = first[to] + val

    write(0, fa)
    coarse(0)
    write(1, fb)
    reorder(result, out, matrix, (slice(None), slice(None)))


def in_vmem(*shape):
    return pltpu.VMEM(shape, jnp.float32)


def order_scratch():
    return pltpu.VMEM((FOLD * LANES, FOLD * LANES), jnp.bfloat16)


def call(kernel, n, ncols, rows, fields, cost, outs, *args, after=(), scratch=()):
    vmem = pl.BlockSpec(memory_space=pltpu.VMEM)
    return pl.pallas_call(
        lambda *refs: kernel(n, *refs[: len(args)], *refs[len(args) + len(after) :]),
        out_shape=outs,
        in_specs=[pl.BlockSpec(memory_space=pltpu.SMEM)] + [vmem] * (len(args) - 1) + [pl.BlockSpec(memory_space=pl.ANY)] * len(after),
        out_specs=[vmem] * len(outs),
        scratch_shapes=[in_vmem(ncols // LANES, rows, LANES)] * fields + list(scratch),
        compiler_params=pltpu.CompilerParams(vmem_limit_bytes=(ncols * rows * fields) * 4 + 6 * 2**20),
        cost_estimate=pl.CostEstimate(flops=cost * 10**6, bytes_accessed=0, transcendentals=0),
    )(*args, *after)


def shards(initial, guess, depth, friction, mask, wind):
    n, ncols = depth.shape
    spaces, times = lax.axis_size("space"), lax.axis_size("tm")
    tm, space = lax.axis_index("tm"), lax.axis_index("space")
    pos = jnp.stack([tm, space]).astype(jnp.int32)
    where = space.astype(jnp.int32)[None]

    def sides(x):
        return lax.ppermute(x, "space", ring(spaces, 1)), lax.ppermute(x, "space", ring(spaces, -1))

    state = in_vmem(3, n, ncols)
    vmem = pl.BlockSpec(memory_space=pltpu.VMEM)
    b_own, last_raw, late_raw = pl.pallas_call(
        functools.partial(main_kernel, n),
        out_shape=(in_vmem(7, n, ncols), state, in_vmem(5, n, ncols)),
        in_specs=[pl.BlockSpec(memory_space=pltpu.HBM)] * 6,
        out_specs=(vmem,) * 3,
        scratch_shapes=[in_vmem(7, n, ncols), pltpu.VMEM((n, ncols), mask.dtype), order_scratch(), pltpu.SemaphoreType.DMA((8,))],
        compiler_params=pltpu.CompilerParams(vmem_limit_bytes=16 * 2**20),
    )(*(pltpu.with_memory_space_constraint(x, pltpu.HBM) for x in (guess, wind, initial, depth, friction, mask)))
    earlier = lax.ppermute(last_raw, "tm", ring(times, 1))
    b_up, b_dn = sides(b_own)
    a_own, last = call(
        late_kernel, n, ncols, 8, 0, 1, (in_vmem(5, n, ncols), state), pos, earlier, last_raw, late_raw, scratch=(in_vmem(5, n, ncols), order_scratch())
    )
    a_up, a_dn = sides(a_own)
    coefs = (b_own, b_up, b_dn)

    (db,) = call(fine_kernel, n, ncols, 120, 8, SWEEP, (state,), where, b_own, b_up, b_dn, *coefs, last)
    db_up, db_dn = sides(db)
    (da,) = call(fine_kernel, n, ncols, 120, 8, SWEEP, (state,), where, a_own, a_up, a_dn, *coefs, b_own, after=(db,))
    da_up, da_dn = sides(da)
    (rb,) = call(relax_b_kernel, n, ncols, 120, 6, SWEEP, (state,), where, db, db_up, db_dn, *coefs, after=(da,))
    ra, fa, fb = call(relax_a_kernel, n, ncols, 120, 6, SWEEP, (state, state, state), where, da, da_up, da_dn, *coefs, db, last, after=(rb,))

    rim = RIMS[2]
    up = lax.ppermute(jnp.concatenate([ra[:, -rim - 2 :], rb[:, -rim:]], axis=1), "space", ring(spaces, 1))
    dn = lax.ppermute(jnp.concatenate([ra[:, : rim + 2], rb[:, :rim]], axis=1), "space", ring(spaces, -1))
    (c1,) = call(source_kernel, n, ncols, 88, 9, 1000, (in_vmem(3, n + 2 * rim, ncols),), pos, ra, rb, up, dn, *coefs)

    ca = lax.ppermute(c1, "tm", ring(times, 1))
    cc = lax.ppermute(c1, "tm", ring(times, -1))
    first, mid, end = rim - RIMS[1], rim + n // 2, rim + n + RIMS[1]
    p1 = lax.ppermute(ca[:, first:mid], "tm", ring(times, 1))
    p2 = lax.ppermute(cc[:, mid:end], "tm", ring(times, -1))
    (out,) = call(
        chain_kernel, n, ncols, 88, 9, SWEEP // 2, (jax.ShapeDtypeStruct(guess.shape, jnp.float32),), pos, ca, cc, p1, p2, *coefs, fa, fb,
        scratch=(in_vmem(*guess.shape), order_scratch()),
    )
    return out


def solution(mesh):
    return jax.shard_map(
        shards,
        mesh=mesh,
        in_specs=(
            P(None, "space", None),
            P("tm", None, "space", None),
            P("space", None),
            P("space", None),
            P("space", None),
            P("tm", None, "space", None),
        ),
        out_specs=P("tm", None, "space", None),
        check_vma=False,
    )
```

```python
import functools

import jax
import jax.numpy as jnp
from jax import lax
from jax.experimental import pallas as pl
from jax.experimental.pallas import tpu as pltpu
from jax.sharding import PartitionSpec as P

FACTOR = 16
H = 0.05
C = 0.5 * H
LANES = 128
SWEEP = 8000


def ring(n, shift):
    return [(i, (i + shift) % n) for i in range(n)]


def at(r, rows=8):
    return pl.ds(r, rows)


FOLD = 4


def diff_cols(chunks):
    lane = lax.broadcasted_iota(jnp.int32, (8, LANES), 1)
    first, last = lane == 0, lane == LANES - 1
    blocks = len(chunks) // FOLD
    left = [pltpu.roll(chunks[b * FOLD + FOLD - 1], 1, 1) for b in range(blocks)]
    right = [pltpu.roll(chunks[b * FOLD], LANES - 1, 1) for b in range(blocks)]
    out = []
    for b in range(blocks):
        for j in range(FOLD):
            c = b * FOLD + j
            lo = chunks[c - 1] if j > 0 else jnp.where(first, left[b - 1] if b > 0 else 0.0, left[b])
            hi = chunks[c + 1] if j < FOLD - 1 else jnp.where(last, right[b + 1] if b + 1 < blocks else 0.0, right[b])
            out.append(hi - lo)
    return out


def order_matrix(inverse):
    size = FOLD * LANES
    place = lax.broadcasted_iota(jnp.int32, (size, size), 0 if inverse else 1)
    column = lax.broadcasted_iota(jnp.int32, (size, size), 1 if inverse else 0)
    return jnp.where(place % LANES * FOLD + place // LANES == column, 1.0, 0.0).astype(jnp.bfloat16)


def reorder(src, dst, matrix, index):
    size = matrix.shape[0]
    for b in range(0, src.shape[-1], size):
        val = src[index + (slice(None), pl.ds(b, size))]
        shape = val.shape
        val = val.reshape(-1, size)
        total = None
        for _ in range(3):
            part = val.astype(jnp.bfloat16)
            val = val - part.astype(jnp.float32)
            piece = jnp.dot(part, matrix[...], preferred_element_type=jnp.float32)
            total = piece if total is None else total + piece
        dst[index + (slice(None), pl.ds(b, size))] = total.reshape(shape)


def copy_in(dst, base, src, index, rows, scale=None):
    for g in range(rows // 8):
        for c in range(dst.shape[0]):
            val = src[index(g) + (pl.ds(c * LANES, LANES),)]
            dst[c, at(pl.multiple_of(base + g * 8, 8)), :] = val if scale is None else val * scale


def plane(f, start=0):
    return lambda g: (f, at(start + g * 8))


def copy_rows(dst, base, src, f, start, rows, scale=1.0):
    for g in range(0, rows, 8):
        count = min(8, rows - g)
        for c in range(dst.shape[0]):
            dst[c, at(base + g, count), :] = src[f, at(start + g, count), pl.ds(c * LANES, LANES)] * scale


def each(fields, base, rows, f):
    def group(g, _):
        for c in range(fields[0].shape[0]):
            f((c, at(base + g * 8), slice(None)))
        return 0

    lax.fori_loop(0, rows // 8, group, 0)


def flux_rows(FY, V, D, base, rows):
    def put(s):
        FY[s] = D[s] * V[s]

    each((FY,), base, rows, put)


def level_pass(E, U, FY, D, r):
    cs = range(E.shape[0])
    dx = diff_cols([D[c, at(r), :] * U[c, at(r), :] for c in cs])
    for c in cs:
        E[c, at(r), :] = E[c, at(r), :] - (dx[c] + (FY[c, at(r + 1), :] - FY[c, at(r - 1), :]))


def velocity_pass(E, U, V, FY, D, A, W, r, gain=None):
    cs = range(E.shape[0])
    dx = diff_cols([E[c, at(r), :] for c in cs])
    for c in cs:
        s = (c, at(r), slice(None))
        dy = E[c, at(r + 1), :] - E[c, at(r - 1), :]
        gx = dx[c]
        if gain is not None:
            gx, dy = gx * gain, dy * gain
        u = A[s] * (U[s] - gx)
        v = A[s] * (V[s] - dy)
        if W is not None:
            u, v = u + W[0][s], v + W[1][s]
        U[s] = u
        V[s] = v
        FY[s] = D[s] * v


def keep_rim(E, base, n, keep):
    for r, k in ((base - 1, keep[0]), (base + n, keep[1])):
        for c in range(E.shape[0]):
            E[c, at(r, 1), :] = E[c, at(r, 1), :] * k


def sweep(E, U, V, FY, D, A, W, base, n, keep):
    for phase in range(FACTOR // 4):
        reach = 2 * FACTOR - 8 * phase
        lo, groups = base - reach, (n + 2 * reach) // 8

        def step(_, carry, lo=lo, groups=groups):
            for g in range(groups):
                level_pass(E, U, FY, D, lo + g * 8)
            keep_rim(E, base, n, keep)
            for g in range(groups):
                velocity_pass(E, U, V, FY, D, A, W, lo + g * 8)
            return carry

        lax.fori_loop(0, 4, step, 0)


def coarse_coefs(D, A, base, rows):
    def put(s):
        D[s] = D[s] * float(FACTOR)
        A[s] = A[s] / (float(FACTOR) - (FACTOR - 1.0) * A[s])

    each((D, A), base, rows, put)


def coarse_step(E, U, V, FY, D, A, lo, rows, base, n, keep):
    for r in range(lo - 1, lo + rows + 1, 8):
        level_pass(E, U, FY, D, r)
    keep_rim(E, base, n, keep)
    for r in range(lo, lo + rows, 8):
        velocity_pass(E, U, V, FY, D, A, None, r, float(FACTOR))


def place(space):
    keep = tuple(jnp.where(x, 1.0, 0.0) for x in (space > 0, space < lax.axis_size("space") - 1))
    return lax.rem(space, 2) == 0, keep, keep[0] * keep[1]


def read_own(src, base, g, c):
    return src[c, at(base + g), :]


def main_kernel(n, guess, wind, initial, depth, friction, mask, out, last, start, raw, land, matrix, sems):
    copies = [
        pltpu.make_async_copy(src, dst, sems.at[i])
        for i, (src, dst) in enumerate(
            (
                (guess.at[0], raw.at[pl.ds(0, 3)]),
                (wind.at[1], raw.at[pl.ds(3, 2)]),
                (depth, raw.at[5]),
                (friction, raw.at[6]),
                (mask, land),
                (wind.at[0], raw.at[pl.ds(7, 2)]),
                (guess.at[1], last),
                (initial, start),
            )
        )
    ]
    for copy in copies:
        copy.start()
    matrix[...] = order_matrix(False)
    for copy in copies:
        copy.wait()
    raw[6] = land[...].astype(jnp.float32) / (1.0 + H * raw[6])
    reorder(raw, out, matrix, (slice(None),))


def last_kernel(n, _, last_raw, last, matrix):
    matrix[...] = order_matrix(False)
    reorder(last_raw, last, matrix, (slice(None),))


def late_kernel(n, pos_ref, earlier, start, out, raw, matrix):
    matrix[...] = order_matrix(False)
    raw[...] = jnp.where(pos_ref[0] == 0, start[...], earlier[...])
    reorder(raw, out, matrix, (slice(None),))


def load(n, base, space, state, coefs, fields, wind=(), first=0):
    E, U, V, D, A = fields
    even, _, inside = place(space)
    rows = (base, jnp.where(even, base - n, base + n), jnp.where(even, base + n, base - n))
    for row, st, cf, ok in zip(rows, state, coefs, (1.0, inside, 1.0)):
        copy_in(D, row, cf, plane(5), n, ok * (C * C))
        copy_in(A, row, cf, plane(6), n, ok)
        copy_in(E, row, st, plane(0), n, C)
        copy_in(U, row, st, plane(1), n)
        copy_in(V, row, st, plane(2), n)
        for k, dst in enumerate(wind):
            copy_in(dst, row, cf, plane(first + k), n, H)


def fine_kernel(wind, n, space_ref, own, across, beside, coef, coef_a, coef_b, nxt, delta, E, U, V, FY, D, A, W0, W1):
    _, keep, _ = place(space_ref[0])
    base = 40
    load(n, base, space_ref[0], (own, across, beside), (coef, coef_a, coef_b), (E, U, V, D, A), (W0, W1), wind)

    def prepare(s):
        W0[s] = W0[s] * A[s]
        W1[s] = W1[s] * A[s]
        FY[s] = D[s] * V[s]

    each((E,), base - n, 3 * n, prepare)
    sweep(E, U, V, FY, D, A, (W0, W1), base, n, keep)
    for f, src in enumerate((E, U, V)):
        for g in range(0, n, 8):
            for c in range(E.shape[0]):
                to = (f, at(g), pl.ds(c * LANES, LANES))
                val = read_own(src, base, g, c)
                if f == 0:
                    val = val * (1.0 / C)
                delta[to] = val - nxt[to]


def relax(n, space_ref, state, coefs, fields):
    E, U, V, FY, D, A = fields
    _, keep, _ = place(space_ref[0])
    base = 40
    load(n, base, space_ref[0], state, coefs, (E, U, V, D, A))
    flux_rows(FY, V, D, base - n, 3 * n)
    sweep(E, U, V, FY, D, A, None, base, n, keep)
    return base


def relax_b_kernel(n, space_ref, d, up, dn, coef, coef_a, coef_b, res, E, U, V, FY, D, A):
    base = relax(n, space_ref, (d, up, dn), (coef, coef_a, coef_b), (E, U, V, FY, D, A))
    copy_out(res, (E, U, V), base, n)


def relax_a_kernel(n, space_ref, d, up, dn, coef, coef_a, coef_b, d_next, nxt, res, fine, next_fine, E, U, V, FY, D, A):
    base = relax(n, space_ref, (d, up, dn), (coef, coef_a, coef_b), (E, U, V, FY, D, A))
    for f, src in enumerate((E, U, V)):
        for g in range(0, n, 8):
            for c in range(E.shape[0]):
                to = (f, at(g), pl.ds(c * LANES, LANES))
                val = read_own(src, base, g, c)
                res[to] = val
                if f == 0:
                    val = val * (1.0 / C)
                fine[to] = d[to] + coef[to]
                next_fine[to] = d_next[to] + nxt[to] + val


def copy_out(dst, src, base, rows):
    for f, field in enumerate(src):
        for g in range(0, rows, 8):
            count = min(8, rows - g)
            for c in range(field.shape[0]):
                dst[f, at(g, count), pl.ds(c * LANES, LANES)] = field[c, at(base + g, count), :]


HALO = 16
RIMS = (2, 6, 10)


def coarse_load(n, base, space, coefs, D, A):
    coef, coef_a, coef_b = coefs
    even, _, inside = place(space)
    for cond, up, dn, ok_up, ok_dn in ((even, coef_a, coef_b, inside, 1.0), (jnp.logical_not(even), coef_b, coef_a, 1.0, inside)):

        @pl.when(cond)
        def _(up=up, dn=dn, ok_up=ok_up, ok_dn=ok_dn):
            for f, dst, k in ((5, D, C * C), (6, A, 1.0)):
                copy_in(dst, base - HALO, up, plane(f, n - HALO), HALO, ok_up * k)
                copy_in(dst, base + n, dn, plane(f), HALO, ok_dn * k)

    copy_in(D, base, coef, plane(5), n, C * C)
    copy_in(A, base, coef, plane(6), n)
    coarse_coefs(D, A, base - HALO, n + 2 * HALO)


def source_kernel(n, pos_ref, ra, rb, up, dn, coef, coef_a, coef_b, out, E, U, V, FY, D, A, X, Y, Z):
    base, rim = 24, RIMS[2]
    _, keep, _ = place(pos_ref[1])
    coarse_load(n, base, pos_ref[1], (coef, coef_a, coef_b), D, A)
    for fields, own, start, rows in (((E, U, V), ra, 0, rim + 2), ((X, Y, Z), rb, rim + 2, rim)):
        for f, dst in enumerate(fields):
            copy_rows(dst, base - rows, up, f, start, rows)
            copy_in(dst, base, own, plane(f), n)
            copy_rows(dst, base + n, dn, f, start, rows)
    flux_rows(FY, V, D, base - HALO, n + 2 * HALO)
    coarse_step(E, U, V, FY, D, A, base - rim, n + 2 * rim, base, n, keep)
    for f, (src, more) in enumerate(((E, X), (U, Y), (V, Z))):
        for g in range(0, n + 2 * rim, 8):
            rows = min(8, n + 2 * rim - g)
            for c in range(E.shape[0]):
                s = (c, at(base - rim + g, rows), slice(None))
                out[f, at(g, rows), pl.ds(c * LANES, LANES)] = src[s] + more[s]


def chain_kernel(n, pos_ref, ca, cc, p1, p2, coef, coef_a, coef_b, fa, fb, out, E, U, V, FY, D, A, X, Y, Z, result, matrix):
    tm = pos_ref[0]
    base, last, middle = 24, RIMS[2], RIMS[1]
    matrix[...] = order_matrix(True)
    _, keep, _ = place(pos_ref[1])
    coarse_load(n, base, pos_ref[1], (coef, coef_a, coef_b), D, A)

    def add():
        def put(s):
            E[s] = E[s] + X[s]
            U[s] = U[s] + Y[s]
            V[s] = V[s] + Z[s]
            FY[s] = D[s] * V[s]

        each((E,), base - 8, n + 16, put)

    def coarse(reach):
        coarse_step(E, U, V, FY, D, A, base - reach, n + 2 * reach, base, n, keep)

    use = jnp.where(tm >= 3, 1.0, 0.0)
    for f, dst in enumerate((E, U, V)):
        copy_rows(dst, base - last, cc, f, 0, n + 2 * last, use)
    flux_rows(FY, V, D, base - HALO, n + 2 * HALO)
    coarse(8)
    coarse(6)
    use = jnp.where(tm >= 2, 1.0, 0.0)
    for f, dst in enumerate((X, Y, Z)):
        copy_rows(dst, base - middle, p1, f, 0, p1.shape[1], use)
        copy_rows(dst, base - middle + p1.shape[1], p2, f, 0, p2.shape[1], use)
    add()
    coarse(4)
    coarse(2)
    use = jnp.where(tm >= 1, 1.0, 0.0)
    for f, dst in enumerate((X, Y, Z)):
        copy_rows(dst, base - last, ca, f, 0, n + 2 * last, use)
    add()

    def write(k, first):
        for f, src in enumerate((E, U, V)):
            for g in range(0, n, 8):
                for c in range(E.shape[0]):
                    to = (f, at(g), pl.ds(c * LANES, LANES))
                    val = read_own(src, base, g, c)
                    if f == 0:
                        val = val * (1.0 / C)
                    result[(k,) + to] = first[to] + val

    write(0, fa)
    coarse(0)
    write(1, fb)
    reorder(result, out, matrix, (slice(None), slice(None)))


def in_vmem(*shape):
    return pltpu.VMEM(shape, jnp.float32)


def order_scratch():
    return pltpu.VMEM((FOLD * LANES, FOLD * LANES), jnp.bfloat16)


def call(kernel, n, ncols, rows, fields, cost, outs, *args, after=(), scratch=()):
    vmem = pl.BlockSpec(memory_space=pltpu.VMEM)
    return pl.pallas_call(
        lambda *refs: kernel(n, *refs[: len(args)], *refs[len(args) + len(after) :]),
        out_shape=outs,
        in_specs=[pl.BlockSpec(memory_space=pltpu.SMEM)] + [vmem] * (len(args) - 1) + [pl.BlockSpec(memory_space=pl.ANY)] * len(after),
        out_specs=[vmem] * len(outs),
        scratch_shapes=[in_vmem(ncols // LANES, rows, LANES)] * fields + list(scratch),
        compiler_params=pltpu.CompilerParams(vmem_limit_bytes=(ncols * rows * fields) * 4 + 6 * 2**20),
        cost_estimate=pl.CostEstimate(flops=cost * 10**6, bytes_accessed=0, transcendentals=0),
    )(*args, *after)


def shards(initial, guess, depth, friction, mask, wind):
    n, ncols = depth.shape
    spaces, times = lax.axis_size("space"), lax.axis_size("tm")
    tm, space = lax.axis_index("tm"), lax.axis_index("space")
    pos = jnp.stack([tm, space]).astype(jnp.int32)
    where = space.astype(jnp.int32)[None]
    even = space % 2 == 0

    def across(x, ends_meet=False):
        if ends_meet:
            return lax.ppermute(x, "space", [(i, (i - 1 if i % 2 == 0 else i + 1) % spaces) for i in range(spaces)])
        pairs = []
        for t in range(times):
            for i in range(spaces):
                other = t * spaces + (i - 1 if i % 2 == 0 else i + 1)
                pairs.append((t * spaces + i, (t ^ 1) * spaces + i if i in (0, spaces - 1) else other))
        return lax.ppermute(x, ("tm", "space"), pairs)

    def beside(x):
        return lax.ppermute(x, "space", [(i, i ^ 1) for i in range(spaces)])

    def sides(x):
        return across(x), beside(x)

    state = in_vmem(3, n, ncols)
    vmem = pl.BlockSpec(memory_space=pltpu.VMEM)
    b_own, last_raw, start = pl.pallas_call(
        functools.partial(main_kernel, n),
        out_shape=(in_vmem(9, n, ncols), state, state),
        in_specs=[pl.BlockSpec(memory_space=pltpu.HBM)] * 6,
        out_specs=(vmem,) * 3,
        scratch_shapes=[in_vmem(9, n, ncols), pltpu.VMEM((n, ncols), mask.dtype), order_scratch(), pltpu.SemaphoreType.DMA((8,))],
        compiler_params=pltpu.CompilerParams(vmem_limit_bytes=16 * 2**20),
    )(*(pltpu.with_memory_space_constraint(x, pltpu.HBM) for x in (guess, wind, initial, depth, friction, mask)))
    earlier = lax.ppermute(last_raw, "tm", ring(times, 1))
    coefs = (b_own, across(b_own, ends_meet=True), beside(b_own))
    (last,) = call(last_kernel, n, ncols, 8, 0, 1, (state,), where, last_raw, scratch=(order_scratch(),))
    (a_own,) = call(late_kernel, n, ncols, 8, 0, 1, (state,), pos, earlier, start, scratch=(state, order_scratch()))
    a_a, a_b = sides(a_own)

    fine_b, fine_a = functools.partial(fine_kernel, 3), functools.partial(fine_kernel, 7)
    (db,) = call(fine_b, n, ncols, 120, 8, SWEEP, (state,), where, *coefs, *coefs, last)
    db_a, db_b = sides(db)
    (da,) = call(fine_a, n, ncols, 120, 8, SWEEP, (state,), where, a_own, a_a, a_b, *coefs, b_own, after=(db,))
    da_a, da_b = sides(da)
    (rb,) = call(relax_b_kernel, n, ncols, 120, 6, SWEEP, (state,), where, db, db_a, db_b, *coefs, after=(da,))
    ra, fa, fb = call(relax_a_kernel, n, ncols, 120, 6, SWEEP, (state, state, state), where, da, da_a, da_b, *coefs, db, last, after=(rb,))

    rim = RIMS[2]
    end = jnp.concatenate([ra[:, -rim - 2 :], rb[:, -rim:]], axis=1)
    top = jnp.concatenate([ra[:, : rim + 2], rb[:, :rim]], axis=1)
    rim_a, rim_b = across(jnp.where(even, top, end)), beside(jnp.where(even, end, top))
    up, dn = jnp.where(even, rim_a, rim_b), jnp.where(even, rim_b, rim_a)
    (c1,) = call(source_kernel, n, ncols, 88, 9, 1000, (in_vmem(3, n + 2 * rim, ncols),), pos, ra, rb, up, dn, *coefs)

    ca = lax.ppermute(c1, "tm", ring(times, 1))
    cc = lax.ppermute(c1, "tm", ring(times, -1))
    first, mid, end = rim - RIMS[1], rim + n // 2, rim + n + RIMS[1]
    p1 = lax.ppermute(ca[:, first:mid], "tm", ring(times, 1))
    p2 = lax.ppermute(cc[:, mid:end], "tm", ring(times, -1))
    (out,) = call(
        chain_kernel, n, ncols, 88, 9, SWEEP // 2, (jax.ShapeDtypeStruct(guess.shape, jnp.float32),), pos, ca, cc, p1, p2, *coefs, fa, fb,
        scratch=(in_vmem(*guess.shape), order_scratch()),
    )
    return out


def solution(mesh):
    return jax.shard_map(
        shards,
        mesh=mesh,
        in_specs=(
            P(None, "space", None),
            P("tm", None, "space", None),
            P("space", None),
            P("space", None),
            P("space", None),
            P("tm", None, "space", None),
        ),
        out_specs=P("tm", None, "space", None),
        check_vma=False,
    )
```

```python
import functools

import jax
import jax.numpy as jnp
from jax import lax
from jax.experimental import pallas as pl
from jax.experimental.pallas import tpu as pltpu
from jax.sharding import PartitionSpec as P

FACTOR = 16
H = 0.05
C = 0.5 * H
LANES = 128
SWEEP = 8000


def ring(n, shift):
    return [(i, (i + shift) % n) for i in range(n)]


def at(r, rows=8):
    return pl.ds(r, rows)


FOLD = 4


def diff_cols(chunks):
    lane = lax.broadcasted_iota(jnp.int32, (8, LANES), 1)
    first, last = lane == 0, lane == LANES - 1
    blocks = len(chunks) // FOLD
    left = [pltpu.roll(chunks[b * FOLD + FOLD - 1], 1, 1) for b in range(blocks)]
    right = [pltpu.roll(chunks[b * FOLD], LANES - 1, 1) for b in range(blocks)]
    out = []
    for b in range(blocks):
        for j in range(FOLD):
            c = b * FOLD + j
            lo = chunks[c - 1] if j > 0 else jnp.where(first, left[b - 1] if b > 0 else 0.0, left[b])
            hi = chunks[c + 1] if j < FOLD - 1 else jnp.where(last, right[b + 1] if b + 1 < blocks else 0.0, right[b])
            out.append(hi - lo)
    return out


def order_matrix(inverse):
    size = FOLD * LANES
    place = lax.broadcasted_iota(jnp.int32, (size, size), 0 if inverse else 1)
    column = lax.broadcasted_iota(jnp.int32, (size, size), 1 if inverse else 0)
    return jnp.where(place % LANES * FOLD + place // LANES == column, 1.0, 0.0).astype(jnp.bfloat16)


def reorder(src, dst, matrix, index):
    size = matrix.shape[0]
    for b in range(0, src.shape[-1], size):
        val = src[index + (slice(None), pl.ds(b, size))]
        shape = val.shape
        val = val.reshape(-1, size)
        total = None
        for _ in range(3):
            part = val.astype(jnp.bfloat16)
            val = val - part.astype(jnp.float32)
            piece = jnp.dot(part, matrix[...], preferred_element_type=jnp.float32)
            total = piece if total is None else total + piece
        dst[index + (slice(None), pl.ds(b, size))] = total.reshape(shape)


def copy_in(dst, base, src, index, rows, scale=None):
    for g in range(rows // 8):
        for c in range(dst.shape[0]):
            val = src[index(g) + (pl.ds(c * LANES, LANES),)]
            dst[c, at(pl.multiple_of(base + g * 8, 8)), :] = val if scale is None else val * scale


def plane(f, start=0):
    return lambda g: (f, at(start + g * 8))


def copy_rows(dst, base, src, f, start, rows, scale=1.0):
    for g in range(0, rows, 8):
        count = min(8, rows - g)
        for c in range(dst.shape[0]):
            dst[c, at(base + g, count), :] = src[f, at(start + g, count), pl.ds(c * LANES, LANES)] * scale


def each(fields, base, rows, f):
    def group(g, _):
        for c in range(fields[0].shape[0]):
            f((c, at(base + g * 8), slice(None)))
        return 0

    lax.fori_loop(0, rows // 8, group, 0)


def flux_rows(FY, V, D, base, rows):
    def put(s):
        FY[s] = D[s] * V[s]

    each((FY,), base, rows, put)


def level_pass(E, U, FY, D, r):
    cs = range(E.shape[0])
    dx = diff_cols([D[c, at(r), :] * U[c, at(r), :] for c in cs])
    for c in cs:
        E[c, at(r), :] = E[c, at(r), :] - (dx[c] + (FY[c, at(r + 1), :] - FY[c, at(r - 1), :]))


def velocity_pass(E, U, V, FY, D, A, W, r, gain=None):
    cs = range(E.shape[0])
    dx = diff_cols([E[c, at(r), :] for c in cs])
    for c in cs:
        s = (c, at(r), slice(None))
        dy = E[c, at(r + 1), :] - E[c, at(r - 1), :]
        gx = dx[c]
        if gain is not None:
            gx, dy = gx * gain, dy * gain
        u = A[s] * (U[s] - gx)
        v = A[s] * (V[s] - dy)
        if W is not None:
            u, v = u + W[0][s], v + W[1][s]
        U[s] = u
        V[s] = v
        FY[s] = D[s] * v


def keep_rim(E, base, n, keep):
    for r, k in ((base - 1, keep[0]), (base + n, keep[1])):
        for c in range(E.shape[0]):
            E[c, at(r, 1), :] = E[c, at(r, 1), :] * k


def sweep(E, U, V, FY, D, A, W, base, n, keep):
    for phase in range(FACTOR // 4):
        reach = 2 * FACTOR - 8 * phase
        lo, groups = base - reach, (n + 2 * reach) // 8

        def step(_, carry, lo=lo, groups=groups):
            for g in range(groups):
                level_pass(E, U, FY, D, lo + g * 8)
            keep_rim(E, base, n, keep)
            for g in range(groups):
                velocity_pass(E, U, V, FY, D, A, W, lo + g * 8)
            return carry

        lax.fori_loop(0, 4, step, 0)


def coarse_coefs(D, A, base, rows):
    def put(s):
        D[s] = D[s] * float(FACTOR)
        A[s] = A[s] / (float(FACTOR) - (FACTOR - 1.0) * A[s])

    each((D, A), base, rows, put)


def coarse_step(E, U, V, FY, D, A, lo, rows, base, n, keep):
    for r in range(lo - 1, lo + rows + 1, 8):
        level_pass(E, U, FY, D, r)
    keep_rim(E, base, n, keep)
    for r in range(lo, lo + rows, 8):
        velocity_pass(E, U, V, FY, D, A, None, r, float(FACTOR))


def place(space):
    keep = tuple(jnp.where(x, 1.0, 0.0) for x in (space > 0, space < lax.axis_size("space") - 1))
    return lax.rem(space, 2) == 0, keep, keep[0] * keep[1]


def read_own(src, base, g, c):
    return src[c, at(base + g), :]


def main_kernel(n, guess, wind, depth, friction, mask, out, last, raw, land, matrix, sems):
    copies = [
        pltpu.make_async_copy(src, dst, sems.at[i])
        for i, (src, dst) in enumerate(
            (
                (guess.at[0], raw.at[pl.ds(0, 3)]),
                (wind.at[1], raw.at[pl.ds(3, 2)]),
                (depth, raw.at[5]),
                (friction, raw.at[6]),
                (mask, land),
                (wind.at[0], raw.at[pl.ds(7, 2)]),
                (guess.at[1], last),
            )
        )
    ]
    for copy in copies:
        copy.start()
    matrix[...] = order_matrix(False)
    for copy in copies:
        copy.wait()
    raw[6] = land[...].astype(jnp.float32) / (1.0 + H * raw[6])
    reorder(raw, out, matrix, (slice(None),))


def last_kernel(last_raw, initial, last, start, raw, matrix, sem):
    copy = pltpu.make_async_copy(initial, raw, sem)
    copy.start()
    matrix[...] = order_matrix(False)
    reorder(last_raw, last, matrix, (slice(None),))
    copy.wait()
    reorder(raw, start, matrix, (slice(None),))


def late_kernel(n, pos_ref, earlier, start, out, matrix):
    matrix[...] = order_matrix(False)
    reorder(earlier, out, matrix, (slice(None),))
    out[...] = jnp.where(pos_ref[0] == 0, start[...], out[...])


def load(n, base, space, state, coefs, fields, wind=(), first=0):
    E, U, V, D, A = fields
    even, _, inside = place(space)
    rows = (base, jnp.where(even, base - n, base + n), jnp.where(even, base + n, base - n))
    for row, st, cf, ok in zip(rows, state, coefs, (1.0, inside, 1.0)):
        copy_in(D, row, cf, plane(5), n, ok * (C * C))
        copy_in(A, row, cf, plane(6), n, ok)
        copy_in(E, row, st, plane(0), n, C)
        copy_in(U, row, st, plane(1), n)
        copy_in(V, row, st, plane(2), n)
        for k, dst in enumerate(wind):
            copy_in(dst, row, cf, plane(first + k), n, H)


def fine_kernel(wind, n, space_ref, own, across, beside, coef, coef_a, coef_b, nxt, delta, E, U, V, FY, D, A, W0, W1):
    _, keep, _ = place(space_ref[0])
    base = 40
    load(n, base, space_ref[0], (own, across, beside), (coef, coef_a, coef_b), (E, U, V, D, A), (W0, W1), wind)

    def prepare(s):
        W0[s] = W0[s] * A[s]
        W1[s] = W1[s] * A[s]
        FY[s] = D[s] * V[s]

    each((E,), base - n, 3 * n, prepare)
    sweep(E, U, V, FY, D, A, (W0, W1), base, n, keep)
    for f, src in enumerate((E, U, V)):
        for g in range(0, n, 8):
            for c in range(E.shape[0]):
                to = (f, at(g), pl.ds(c * LANES, LANES))
                val = read_own(src, base, g, c)
                if f == 0:
                    val = val * (1.0 / C)
                delta[to] = val - nxt[to]


def relax(n, space_ref, state, coefs, fields):
    E, U, V, FY, D, A = fields
    _, keep, _ = place(space_ref[0])
    base = 40
    load(n, base, space_ref[0], state, coefs, (E, U, V, D, A))
    flux_rows(FY, V, D, base - n, 3 * n)
    sweep(E, U, V, FY, D, A, None, base, n, keep)
    return base


def relax_b_kernel(n, space_ref, d, up, dn, coef, coef_a, coef_b, res, E, U, V, FY, D, A):
    base = relax(n, space_ref, (d, up, dn), (coef, coef_a, coef_b), (E, U, V, FY, D, A))
    copy_out(res, (E, U, V), base, n)


def relax_a_kernel(n, space_ref, d, up, dn, coef, coef_a, coef_b, d_next, nxt, res, fine, next_fine, E, U, V, FY, D, A):
    base = relax(n, space_ref, (d, up, dn), (coef, coef_a, coef_b), (E, U, V, FY, D, A))
    for f, src in enumerate((E, U, V)):
        for g in range(0, n, 8):
            for c in range(E.shape[0]):
                to = (f, at(g), pl.ds(c * LANES, LANES))
                val = read_own(src, base, g, c)
                res[to] = val
                if f == 0:
                    val = val * (1.0 / C)
                fine[to] = d[to] + coef[to]
                next_fine[to] = d_next[to] + nxt[to] + val


def copy_out(dst, src, base, rows):
    for f, field in enumerate(src):
        for g in range(0, rows, 8):
            count = min(8, rows - g)
            for c in range(field.shape[0]):
                dst[f, at(g, count), pl.ds(c * LANES, LANES)] = field[c, at(base + g, count), :]


HALO = 16
RIMS = (2, 6, 10)


def coarse_load(n, base, space, coefs, D, A):
    coef, coef_a, coef_b = coefs
    even, _, inside = place(space)
    for cond, up, dn, ok_up, ok_dn in ((even, coef_a, coef_b, inside, 1.0), (jnp.logical_not(even), coef_b, coef_a, 1.0, inside)):

        @pl.when(cond)
        def _(up=up, dn=dn, ok_up=ok_up, ok_dn=ok_dn):
            for f, dst, k in ((5, D, C * C), (6, A, 1.0)):
                copy_in(dst, base - HALO, up, plane(f, n - HALO), HALO, ok_up * k)
                copy_in(dst, base + n, dn, plane(f), HALO, ok_dn * k)

    copy_in(D, base, coef, plane(5), n, C * C)
    copy_in(A, base, coef, plane(6), n)
    coarse_coefs(D, A, base - HALO, n + 2 * HALO)


def source_kernel(n, pos_ref, ra, rb, up, dn, coef, coef_a, coef_b, out, E, U, V, FY, D, A, X, Y, Z):
    base, rim = 24, RIMS[2]
    _, keep, _ = place(pos_ref[1])
    coarse_load(n, base, pos_ref[1], (coef, coef_a, coef_b), D, A)
    for fields, own, start, rows in (((E, U, V), ra, 0, rim + 2), ((X, Y, Z), rb, rim + 2, rim)):
        for f, dst in enumerate(fields):
            copy_rows(dst, base - rows, up, f, start, rows)
            copy_in(dst, base, own, plane(f), n)
            copy_rows(dst, base + n, dn, f, start, rows)
    flux_rows(FY, V, D, base - HALO, n + 2 * HALO)
    coarse_step(E, U, V, FY, D, A, base - rim, n + 2 * rim, base, n, keep)
    for f, (src, more) in enumerate(((E, X), (U, Y), (V, Z))):
        for g in range(0, n + 2 * rim, 8):
            rows = min(8, n + 2 * rim - g)
            for c in range(E.shape[0]):
                s = (c, at(base - rim + g, rows), slice(None))
                out[f, at(g, rows), pl.ds(c * LANES, LANES)] = src[s] + more[s]


def chain_kernel(n, pos_ref, ca, cc, p1, p2, coef, coef_a, coef_b, fa, fb, out, E, U, V, FY, D, A, X, Y, Z, result, matrix):
    tm = pos_ref[0]
    base, last, middle = 24, RIMS[2], RIMS[1]
    matrix[...] = order_matrix(True)
    _, keep, _ = place(pos_ref[1])
    coarse_load(n, base, pos_ref[1], (coef, coef_a, coef_b), D, A)

    def add():
        def put(s):
            E[s] = E[s] + X[s]
            U[s] = U[s] + Y[s]
            V[s] = V[s] + Z[s]
            FY[s] = D[s] * V[s]

        each((E,), base - 8, n + 16, put)

    def coarse(reach):
        coarse_step(E, U, V, FY, D, A, base - reach, n + 2 * reach, base, n, keep)

    use = jnp.where(tm >= 3, 1.0, 0.0)
    for f, dst in enumerate((E, U, V)):
        copy_rows(dst, base - last, cc, f, 0, n + 2 * last, use)
    flux_rows(FY, V, D, base - HALO, n + 2 * HALO)
    coarse(8)
    coarse(6)
    use = jnp.where(tm >= 2, 1.0, 0.0)
    for f, dst in enumerate((X, Y, Z)):
        copy_rows(dst, base - middle, p1, f, 0, p1.shape[1], use)
        copy_rows(dst, base - middle + p1.shape[1], p2, f, 0, p2.shape[1], use)
    add()
    coarse(4)
    coarse(2)
    use = jnp.where(tm >= 1, 1.0, 0.0)
    for f, dst in enumerate((X, Y, Z)):
        copy_rows(dst, base - last, ca, f, 0, n + 2 * last, use)
    add()

    def write(k, first):
        for f, src in enumerate((E, U, V)):
            for g in range(0, n, 8):
                for c in range(E.shape[0]):
                    to = (f, at(g), pl.ds(c * LANES, LANES))
                    val = read_own(src, base, g, c)
                    if f == 0:
                        val = val * (1.0 / C)
                    result[(k,) + to] = first[to] + val

    write(0, fa)
    coarse(0)
    write(1, fb)
    reorder(result, out, matrix, (slice(None), slice(None)))


def in_vmem(*shape):
    return pltpu.VMEM(shape, jnp.float32)


def order_scratch():
    return pltpu.VMEM((FOLD * LANES, FOLD * LANES), jnp.bfloat16)


def call(kernel, n, ncols, rows, fields, cost, outs, *args, after=(), scratch=()):
    vmem = pl.BlockSpec(memory_space=pltpu.VMEM)
    return pl.pallas_call(
        lambda *refs: kernel(n, *refs[: len(args)], *refs[len(args) + len(after) :]),
        out_shape=outs,
        in_specs=[pl.BlockSpec(memory_space=pltpu.SMEM)] + [vmem] * (len(args) - 1) + [pl.BlockSpec(memory_space=pl.ANY)] * len(after),
        out_specs=[vmem] * len(outs),
        scratch_shapes=[in_vmem(ncols // LANES, rows, LANES)] * fields + list(scratch),
        compiler_params=pltpu.CompilerParams(vmem_limit_bytes=(ncols * rows * fields) * 4 + 6 * 2**20),
        cost_estimate=pl.CostEstimate(flops=cost * 10**6, bytes_accessed=0, transcendentals=0),
    )(*args, *after)


def shards(initial, guess, depth, friction, mask, wind):
    n, ncols = depth.shape
    spaces, times = lax.axis_size("space"), lax.axis_size("tm")
    tm, space = lax.axis_index("tm"), lax.axis_index("space")
    pos = jnp.stack([tm, space]).astype(jnp.int32)
    where = space.astype(jnp.int32)[None]
    even = space % 2 == 0

    def across(x, ends_meet=False):
        if ends_meet:
            return lax.ppermute(x, "space", [(i, (i - 1 if i % 2 == 0 else i + 1) % spaces) for i in range(spaces)])
        pairs = []
        for t in range(times):
            for i in range(spaces):
                other = t * spaces + (i - 1 if i % 2 == 0 else i + 1)
                pairs.append((t * spaces + i, (t ^ 1) * spaces + i if i in (0, spaces - 1) else other))
        return lax.ppermute(x, ("tm", "space"), pairs)

    def beside(x):
        return lax.ppermute(x, "space", [(i, i ^ 1) for i in range(spaces)])

    def sides(x):
        return across(x), beside(x)

    state = in_vmem(3, n, ncols)
    vmem = pl.BlockSpec(memory_space=pltpu.VMEM)
    hbm = pl.BlockSpec(memory_space=pltpu.HBM)
    params = pltpu.CompilerParams(vmem_limit_bytes=16 * 2**20)

    def in_hbm(*args):
        return [pltpu.with_memory_space_constraint(x, pltpu.HBM) for x in args]

    b_own, last_raw = pl.pallas_call(
        functools.partial(main_kernel, n),
        out_shape=(in_vmem(9, n, ncols), state),
        in_specs=[hbm] * 5,
        out_specs=(vmem,) * 2,
        scratch_shapes=[in_vmem(9, n, ncols), pltpu.VMEM((n, ncols), mask.dtype), order_scratch(), pltpu.SemaphoreType.DMA((7,))],
        compiler_params=params,
    )(*in_hbm(guess, wind, depth, friction, mask))
    earlier = lax.ppermute(last_raw, "tm", ring(times, 1))
    coefs = (b_own, across(b_own, ends_meet=True), beside(b_own))
    last, start = pl.pallas_call(
        last_kernel,
        out_shape=(state, state),
        in_specs=[vmem, hbm],
        out_specs=(vmem,) * 2,
        scratch_shapes=[state, order_scratch(), pltpu.SemaphoreType.DMA],
        compiler_params=params,
    )(last_raw, *in_hbm(initial))
    (a_own,) = call(late_kernel, n, ncols, 8, 0, 1, (state,), pos, earlier, start, scratch=(order_scratch(),))
    a_a, a_b = sides(a_own)

    fine_b, fine_a = functools.partial(fine_kernel, 3), functools.partial(fine_kernel, 7)
    (db,) = call(fine_b, n, ncols, 120, 8, SWEEP, (state,), where, *coefs, *coefs, last)
    db_a, db_b = sides(db)
    (da,) = call(fine_a, n, ncols, 120, 8, SWEEP, (state,), where, a_own, a_a, a_b, *coefs, b_own, after=(db,))
    da_a, da_b = sides(da)
    (rb,) = call(relax_b_kernel, n, ncols, 120, 6, SWEEP, (state,), where, db, db_a, db_b, *coefs, after=(da,))
    ra, fa, fb = call(relax_a_kernel, n, ncols, 120, 6, SWEEP, (state, state, state), where, da, da_a, da_b, *coefs, db, last, after=(rb,))

    rim = RIMS[2]
    end = jnp.concatenate([ra[:, -rim - 2 :], rb[:, -rim:]], axis=1)
    top = jnp.concatenate([ra[:, : rim + 2], rb[:, :rim]], axis=1)
    rim_a, rim_b = across(jnp.where(even, top, end)), beside(jnp.where(even, end, top))
    up, dn = jnp.where(even, rim_a, rim_b), jnp.where(even, rim_b, rim_a)
    (c1,) = call(source_kernel, n, ncols, 88, 9, 1000, (in_vmem(3, n + 2 * rim, ncols),), pos, ra, rb, up, dn, *coefs)

    ca = lax.ppermute(c1, "tm", ring(times, 1))
    cc = lax.ppermute(c1, "tm", ring(times, -1))
    first, mid, end = rim - RIMS[1], rim + n // 2, rim + n + RIMS[1]
    p1 = lax.ppermute(ca[:, first:mid], "tm", ring(times, 1))
    p2 = lax.ppermute(cc[:, mid:end], "tm", ring(times, -1))
    (out,) = call(
        chain_kernel, n, ncols, 88, 9, SWEEP // 2, (jax.ShapeDtypeStruct(guess.shape, jnp.float32),), pos, ca, cc, p1, p2, *coefs, fa, fb,
        scratch=(in_vmem(*guess.shape), order_scratch()),
    )
    return out


def solution(mesh):
    return jax.shard_map(
        shards,
        mesh=mesh,
        in_specs=(
            P(None, "space", None),
            P("tm", None, "space", None),
            P("space", None),
            P("space", None),
            P("space", None),
            P("tm", None, "space", None),
        ),
        out_specs=P("tm", None, "space", None),
        check_vma=False,
    )
```
